256 devices in a mesh: front: 8 (over y, x_lo), row: 4 (over x_hi, core), col: 8 (over z).
Axes of the slice: x: 4 (x_hi: 2, x_lo: 2; x = x_hi * 2 + x_lo), y: 4, z: 8, core: 2. Of those that a mesh axis runs over, the one named last changes fastest.
Arguments:
- front_slab: float32 [8, 32, 4, 128, 1, 8, 256], P('front', None, 'row', None, None, 'col'), as said below
- child_keep: float32 [8, 8, 4, 128, 1, 8, 256], P('front', None, 'row', None, None, 'col'), may hold values from -1 to 1
- child_give: float32 [8, 8, 4, 128, 1, 8, 256], P('front', None, 'row', None, None, 'col'), may hold values from -1 to 1
- map_keep: int32 [8, 8, 4], replicated, may hold values from 0 to 127, as said below
- map_give: int32 [8, 8, 4], replicated, may hold values from 0 to 127, as said below
Outputs:
- factored: float32 [8, 32, 4, 128, 1, 8, 256], P('front', None, 'row', None, None, 'col')
The draws below stay inside these ranges and needn't reach their ends.
Inputs may be any that keep to these rules, and one draw needn't show every extreme that they name: `map_keep`: row blocks of one child map to distinct parent row blocks. Parent row block p is held by row index p mod 4. Of the child row blocks held by one row index, at most 4 map to blocks held by any one row index, and every row index sends exactly 4 of them to one row index. `map_give`: as for map_keep, for the child held by each front's devices. `front_slab`: the leading 256 x 256 block of every front, after the children are added, is symmetric-part diagonally dominant with a positive diagonal.
All inputs are finite; a program needn't handle non-finite values.
Results may differ from the reference program's by a relative error of at most 0.0001.
Values sent between devices are 32-bit elements; how exact they have to be, the bound alone decides.
A program may use at most 128 MiB of HBM per device.

```python
import jax
import jax.numpy as jnp
from jax import lax

NF = 16384
BLK = 128
PANEL = 256
CHILD = 4096
CBL = 1
FRONTS = 8
RBL = 32
UBR = 8
N_ROW = 4
N_COL = 8


def child_table(key):
    groups = N_ROW
    capacity = UBR // 2
    blocks = NF // (BLK * N_ROW)
    key_offset, key_order, key_extra, key_place = jax.random.split(key, 4)
    offset = jax.random.randint(key_offset, (groups,), 0, groups)
    order = jax.vmap(lambda sub: jax.random.permutation(sub, UBR))(jax.random.split(key_order, groups))
    extra = jax.random.randint(key_extra, (groups, UBR), 0, groups - 1)
    source = jnp.arange(groups, dtype=jnp.int32)[:, None]
    target = jnp.where(order < capacity, (source + offset[:, None]) % groups, (source + offset[:, None] + 1 + extra) % groups)
    flat = target.reshape(-1)
    markers = (flat[:, None] == jnp.arange(groups, dtype=jnp.int32)[None, :]).astype(jnp.int32)
    before = jnp.cumsum(markers, axis=0) - markers
    ranked = jnp.sum(before * markers, axis=1)
    choices_of = jax.vmap(lambda sub: jax.random.permutation(sub, blocks))(jax.random.split(key_place, groups))
    position = choices_of[flat, ranked]
    parent = (position * groups + flat).reshape(groups, UBR)
    return parent.T.astype(jnp.int32)


def draw_map_keep(key, part):
    key = jax.random.fold_in(key, 11)
    return jax.vmap(child_table)(jax.random.split(key, FRONTS))


def draw_map_give(key, part):
    key = jax.random.fold_in(key, 23)
    return jax.vmap(child_table)(jax.random.split(key, FRONTS))


def draw_front_slab(key, part):
    key = jax.random.fold_in(key, 5)
    shape = (FRONTS, RBL, N_ROW, BLK, CBL, N_COL, PANEL)
    base = jax.random.uniform(key, shape, jnp.float32, -1.0, 1.0)
    row_index = (lax.broadcasted_iota(jnp.int32, shape, 1) * N_ROW + lax.broadcasted_iota(jnp.int32, shape, 2)) * BLK + lax.broadcasted_iota(jnp.int32, shape, 3)
    col_index = (lax.broadcasted_iota(jnp.int32, shape, 4) * N_COL + lax.broadcasted_iota(jnp.int32, shape, 5)) * PANEL + lax.broadcasted_iota(jnp.int32, shape, 6)
    factor = jnp.where(col_index < PANEL, jnp.where(row_index >= PANEL, 5.0, 1.0), 1.7)
    boost = jnp.where((row_index == col_index) & (col_index < PANEL), 3.2 * PANEL, 0.0)
    return (base * factor + boost).astype(jnp.float32)


def block_scale(stream_key, shape, shards, least, top_value):
    loudness = 1.0
    for dim, parts in shards:
        draws = jax.random.uniform(jax.random.fold_in(jax.random.fold_in(stream_key, 6), dim), (parts,), jnp.float32, least / len(shards), top_value / len(shards))
        loudness = loudness * jnp.repeat(jnp.exp(draws), shape[dim] // parts).reshape((-1,) + (1,) * (len(shape) - 1 - dim))
    return loudness


def setup_inputs(seed: int = 0) -> dict:
    splits = jax.random.split(jax.random.key(seed), 6)
    front_slab = draw_front_slab(jax.random.fold_in(splits[5], 71), 0)
    child_keep = jnp.clip(jax.random.uniform(splits[1], (FRONTS, UBR, N_ROW, BLK, CBL, N_COL, PANEL), jnp.float32, -1.0, 1.0) * block_scale(splits[1], (FRONTS, UBR, N_ROW, BLK, CBL, N_COL, PANEL), ((0, 8), (2, 4), (5, 8)), -0.4, 0.0), -1.0, 1.0)
    child_give = jnp.clip(jax.random.uniform(splits[2], (FRONTS, UBR, N_ROW, BLK, CBL, N_COL, PANEL), jnp.float32, -1.0, 1.0) * block_scale(splits[2], (FRONTS, UBR, N_ROW, BLK, CBL, N_COL, PANEL), ((0, 8), (2, 4), (5, 8)), -0.4, 0.0), -1.0, 1.0)
    map_keep = draw_map_keep(jax.random.fold_in(splits[5], 71), 0)
    map_give = draw_map_give(jax.random.fold_in(splits[5], 71), 0)
    return dict(front_slab=front_slab, child_keep=child_keep, child_give=child_give, map_keep=map_keep, map_give=map_give)


def extend_rows(matrix, child, table):
    stacked = matrix.reshape(-1, BLK, matrix.shape[1])
    pieces = child.reshape(-1, BLK, matrix.shape[1])
    stacked = stacked.at[table.reshape(-1).astype(jnp.int32)].add(pieces)
    return stacked.reshape(matrix.shape)

def assemble_front(slab, kept, moved, kept_map, moved_map):
    slab_width = CBL * N_COL * PANEL
    matrix = slab.reshape(NF, slab_width)
    matrix = extend_rows(matrix, kept.reshape(CHILD, slab_width), kept_map)
    matrix = extend_rows(matrix, moved.reshape(CHILD, slab_width), moved_map)
    lower_factor = jnp.linalg.cholesky(matrix[:PANEL, :PANEL])
    solved = lax.linalg.triangular_solve(lower_factor, matrix[:, :PANEL], left_side=False, lower=True, transpose_a=True)
    row_index = jnp.arange(NF)
    leading = jnp.take(lower_factor, jnp.minimum(row_index, PANEL - 1), axis=0)
    panel = jnp.where(row_index[:, None] < PANEL, leading, solved)
    update = jnp.dot(panel, panel[PANEL:slab_width].T, precision=lax.Precision.HIGHEST)
    trailing = jnp.where(row_index[:, None] < PANEL, jnp.float32(0.0), matrix[:, PANEL:] - update)
    return jnp.concatenate([panel, trailing], axis=1).reshape(slab.shape)

def reference(front_slab, child_keep, child_give, map_keep, map_give):
    results = []
    for front_number in range(FRONTS):
        partner = front_number ^ 1
        results.append(assemble_front(front_slab[front_number], child_keep[front_number], child_give[partner], map_keep[front_number], map_give[partner]))
    return jnp.stack(results)
```

```python
import functools

import jax
import jax.numpy as jnp
from jax import lax
from jax.experimental import pallas as pl
from jax.experimental.pallas import tpu as pltpu
from jax.sharding import PartitionSpec as P

F32 = jnp.float32
BF16 = jnp.bfloat16
precise = lax.Precision.HIGHEST

CHUNKS = (8, 8, 16, 16, 16, 16, 16, 16, 16)
STARTS = tuple(sum(CHUNKS[:i]) for i in range(len(CHUNKS)))
NCH = len(CHUNKS)
WINDOW = 3
PARTS = 32
SKEW = 2


def place():
    front = lax.axis_index("front")
    row = lax.axis_index("row")
    col = lax.axis_index("col")
    x = (row // 2) * 2 + front % 2
    return x, front // 2, col, row % 2


def device(x, y, z, core):
    x = lax.rem(x + 4, 4)
    z = lax.rem(z + 8, 8)
    return {"front": y * 2 + x % 2, "row": (x // 2) * 2 + core, "col": z}


def row_of(x, core):
    return (lax.rem(x + 4, 4) // 2) * 2 + core


def exchange_kernel(
    inv,
    front_hbm,
    keep_hbm,
    give_hbm,
    panel_out,
    slab_out,
    window_out,
    slab,
    panel,
    win,
    load_sem,
    own_sem,
    xs,
    xr,
    ms,
    mr,
    zs,
    zr,
    ws,
    wr,
    out_sem,
    *pools,
):
    x, y, z, core = place()
    row = row_of(x, core)
    mate = device(x, y, z, 1 - core)
    far = device(x + 2, y, z, core)
    far_mate = device(x + 2, y, z, 1 - core)
    up = device(x + 1, y, z, core)
    down = device(x - 1, y, z, core)
    nxt = device(x, y, z + 1, core)
    prv = device(x, y, z - 1, core)
    row_far = lax.rem(row + 2, 4)
    row_mate = row_of(x, 1 - core)
    row_mate_far = lax.rem(row_mate + 2, 4)
    row_up = row_of(x + 1, core)
    row_down = row_of(x - 1, core)
    row_up_mate = row_of(x + 1, 1 - core)
    row_down_mate = row_of(x - 1, 1 - core)

    load = pltpu.make_async_copy(front_hbm, slab, load_sem)
    load.start()

    barrier = pltpu.get_barrier_semaphore()
    for target in (mate, far, far_mate, up, down, nxt, prv):
        pl.semaphore_signal(barrier, 1, device_id=target)
    pl.semaphore_wait(barrier, 7)

    def rows(j):
        return pl.ds(2 * STARTS[j], 2 * CHUNKS[j])

    def eight(base):
        return pl.ds(base, 8)

    def remote(src, dst, s, r, dev):
        return pltpu.make_async_remote_copy(src, dst, s, r, device_id=dev)

    def send_x(j):
        pool = pools[j]
        keep = keep_hbm.at[:, rows(j)]
        give = give_hbm.at[:, rows(j)]
        mine = pool.at[eight(8 * row)]
        given = pool.at[eight(32 + 8 * row)]
        return (
            remote(keep, mine, xs.at[0, j], xr.at[0, j], far),
            remote(give, given, xs.at[1, j], xr.at[1, j], up),
            remote(give, given, xs.at[2, j], xr.at[2, j], down),
        )

    def recv_x(j):
        pool = pools[j]
        give = give_hbm.at[:, rows(j)]
        return (
            remote(give, pool.at[eight(8 * row_far)], xs.at[0, j], xr.at[0, j], far),
            remote(give, pool.at[eight(32 + 8 * row_down)], xs.at[1, j], xr.at[1, j], down),
            remote(give, pool.at[eight(32 + 8 * row_up)], xs.at[2, j], xr.at[2, j], up),
        )

    def own_copy(j):
        return pltpu.make_async_copy(
            keep_hbm.at[:, rows(j)], pools[j].at[eight(8 * row)], own_sem.at[j]
        )

    def own_relay(j):
        mine = pools[j].at[eight(8 * row)]
        return remote(keep_hbm.at[:, rows(j)], mine, ms.at[0, j], mr.at[0, j], mate)

    def relays(j):
        out = []
        for p, base in ((1, 8 * row_far), (2, 32 + 8 * row_down), (3, 32 + 8 * row_up)):
            part = pools[j].at[eight(base)]
            out.append(remote(part, part, ms.at[p, j], mr.at[p, j], mate))
        return out

    def relayed(j):
        out = []
        for p, base in (
            (0, 8 * row_mate),
            (1, 8 * row_mate_far),
            (2, 32 + 8 * row_down_mate),
            (3, 32 + 8 * row_up_mate),
        ):
            part = pools[j].at[eight(base)]
            out.append(remote(part, part, ms.at[p, j], mr.at[p, j], mate))
        return out

    def begin_x(j):
        for c in send_x(j):
            c.start()
        own_copy(j).start()
        own_relay(j).start()

    def arrive_x(j):
        for c in recv_x(j):
            c.wait_recv()
        for c in relays(j):
            c.start()

    def assemble(j):
        own_copy(j).wait()
        for c in relayed(j):
            c.wait_recv()
        pool = pools[j]

        def one(b, carry):
            kept = pool[inv[b]]
            moved = pool[inv[32 + b]]
            slab[b, rows(j), :] = slab[b, rows(j), :] + kept + moved
            return carry

        lax.fori_loop(0, 32, one, 0, unroll=4)

    def part(ref, way, t):
        j8 = t // 2
        g = t % 2
        return ref.at[pl.ds(16 * way + 8 * g, 8), pl.ds(pl.multiple_of(16 * j8, 16), 16)]

    def hop(ref, way, t):
        return remote(
            part(ref, way, t),
            part(panel, way, t),
            zs.at[way, t],
            zr.at[way, t],
            prv if way else nxt,
        )

    for j in range(NCH):
        pools[j][64] = jnp.zeros(pools[j].shape[1:], F32)
    for j in range(WINDOW):
        begin_x(j)
    load.wait()

    @pl.when(z == 0)
    def _():
        for j in range(NCH):
            arrive_x(j)
            if j + WINDOW < NCH:
                begin_x(j + WINDOW)
            assemble(j)

            def launch(t, carry):
                for way in (0, 1):
                    hop(slab, way, t).start()
                return carry

            lax.fori_loop(STARTS[j] // 4, (STARTS[j] + CHUNKS[j]) // 4, launch, 0)

    @pl.when(z != 0)
    def _():
        total = PARTS + SKEW * 6

        def step(s, carry):
            for way in (0, 1):
                lag = (7 - z) if way else (z - 1)
                t = s - SKEW * lag

                @pl.when((t >= 0) & (t < PARTS))
                def _():
                    copy = hop(panel, way, t)
                    copy.wait_recv()

                    @pl.when(lag < 6)
                    def _():
                        copy.start()

            return carry

        done = 0
        for j in range(NCH):
            until = 4 + 4 * j
            lax.fori_loop(done, until, step, 0)
            done = until
            arrive_x(j)
            if j + WINDOW < NCH:
                begin_x(j + WINDOW)
            if j:
                assemble(j - 1)
        lax.fori_loop(done, total, step, 0)
        assemble(NCH - 1)

    half = z // 2
    owner = 2 * lax.rem(z, 2)

    def spread(ref, block, slot):
        src = ref.at[block]
        out = []
        for i, dev in enumerate((mate, far, far_mate)):
            out.append(remote(src, win.at[slot], ws.at[slot // 2, i], wr.at[slot], dev))
        return out

    def share(ref):
        @pl.when(row < 2)
        def _():
            win[row] = ref[0]
            for slot in (0, 1):

                @pl.when(row == slot)
                def _():
                    for c in spread(ref, 0, slot):
                        c.start()

        for h in (0, 1):

            @pl.when(row == owner + h)
            def _():
                win[2 + h] = ref[half]
                for c in spread(ref, half, 2 + h):
                    c.start()

    @pl.when(z == 0)
    def _():
        share(slab)
        pltpu.make_async_copy(slab, panel_out, out_sem.at[0]).start()

    @pl.when(z != 0)
    def _():
        share(panel)
        pltpu.make_async_copy(panel, panel_out, out_sem.at[0]).start()

    pltpu.make_async_copy(slab, slab_out, out_sem.at[1]).start()

    for slot in range(4):
        holder = slot if slot < 2 else owner + slot - 2

        @pl.when(row != holder)
        def _():
            remote(win.at[slot], win.at[slot], ws.at[0, 0], wr.at[slot], mate).wait_recv()

    pltpu.make_async_copy(win, window_out, out_sem.at[2]).start()

    for slot in range(4):
        holder = slot if slot < 2 else owner + slot - 2

        @pl.when(row == holder)
        def _():
            for c in spread(panel, 0, slot):
                c.wait_send()

    for j in range(NCH):
        for c in send_x(j):
            c.wait_send()
        own_relay(j).wait_send()
        for c in relays(j):
            c.wait_send()

    def drain(t, carry):
        for way in (0, 1):
            last = 1 if way else 7

            @pl.when(z != last)
            def _():
                hop(panel, way, t).wait_send()

        return carry

    lax.fori_loop(0, PARTS, drain, 0)
    pltpu.make_async_copy(panel, panel_out, out_sem.at[0]).wait()
    pltpu.make_async_copy(slab, slab_out, out_sem.at[1]).wait()
    pltpu.make_async_copy(win, window_out, out_sem.at[2]).wait()


def exchange(inv, front, keep, give):
    big = jax.ShapeDtypeStruct(front.shape, F32)
    anywhere = pl.BlockSpec(memory_space=pl.ANY)
    dma = pltpu.SemaphoreType.DMA
    return pl.pallas_call(
        exchange_kernel,
        out_shape=[big, big, jax.ShapeDtypeStruct((4, 256, 128), F32)],
        in_specs=[pl.BlockSpec(memory_space=pltpu.SMEM)] + [anywhere] * 3,
        out_specs=[anywhere] * 3,
        scratch_shapes=[
            pltpu.VMEM(front.shape, F32),
            pltpu.VMEM(front.shape, F32),
            pltpu.VMEM((4, 256, 128), F32),
            dma,
            dma((NCH,)),
            dma((3, NCH)),
            dma((3, NCH)),
            dma((4, NCH)),
            dma((4, NCH)),
            dma((2, PARTS)),
            dma((2, PARTS)),
            dma((2, 3)),
            dma((4,)),
            dma((3,)),
        ]
        + [pltpu.VMEM((65, 2 * n, 128), F32) for n in CHUNKS],
        compiler_params=pltpu.CompilerParams(
            collective_id=0, has_side_effects=True, vmem_limit_bytes=56 << 20
        ),
        name="exchange",
    )(inv, front, keep, give)


def three(a):
    hi = a.astype(BF16)
    rest = a - hi.astype(F32)
    mid = rest.astype(BF16)
    low = (rest - mid.astype(F32)).astype(BF16)
    return hi, mid, low


def factor_panel(work, upper, j0, n=16):
    r = work[j0 : j0 + n, :]
    sub = lax.broadcasted_iota(jnp.int32, (n, 128), 0)
    sub2 = lax.broadcasted_iota(jnp.int32, (n, 256), 0)
    lane2 = lax.broadcasted_iota(jnp.int32, (n, 256), 1)
    g = [jnp.broadcast_to(r[:, j0 + i : j0 + i + 1], (n, 128)) for i in range(n)]
    for i in range(n):
        inv = lax.rsqrt(g[i][i : i + 1, :])
        l = g[i] * inv
        below = jnp.where(sub > i, l, 0.0)
        for m in range(i + 1, n):
            g[m] = g[m] - below * l[m : m + 1, :]
        line = r[i : i + 1, :] * jnp.concatenate([inv, inv], axis=1)
        r = jnp.where(sub2 == i, line, r - jnp.concatenate([below, below], axis=1) * line)
    r = jnp.where(lane2 >= sub2 + j0, r, 0.0)
    upper[j0 : j0 + n, :] = r
    if j0 + n < 256:
        h, m, l = three(r)
        a = jnp.concatenate([h, h, m, h, l, m], axis=0)
        b = jnp.concatenate([h, m, h, l, h, m], axis=0)
        t = lax.dot_general(a, b, (((0,), (0,)), ((), ())), preferred_element_type=F32)
        work[j0 + n :, :] = work[j0 + n :, :] - t[j0 + n :, :]


def invert_upper(u):
    i = lax.broadcasted_iota(jnp.int32, (256, 256), 0)
    j = lax.broadcasted_iota(jnp.int32, (256, 256), 1)
    inv = jnp.where(i == j, 1.0 / jnp.where(i == j, u, 1.0), 0.0)
    s = 1
    while s < 256:
        off = jnp.where((i // (2 * s) == j // (2 * s)) & (i // s < j // s), u, 0.0)
        step = jnp.dot(inv, off, precision=precise, preferred_element_type=F32)
        inv = inv - jnp.dot(step, inv, precision=precise, preferred_element_type=F32)
        s *= 2
    return inv


def square(ref, a, b):
    even, odd = pl.ds(0, 128, 2), pl.ds(1, 128, 2)
    top = jnp.concatenate([ref[a, even, :], ref[a, odd, :]], axis=1)
    low = jnp.concatenate([ref[b, even, :], ref[b, odd, :]], axis=1)
    return jnp.concatenate([top, low], axis=0)


def factor_kernel(ids, win, weight, top, work, upper):
    lead = square(win, 0, 1)
    work[...] = 0.5 * (lead + lead.T)
    for p in range(16):
        factor_panel(work, upper, 16 * p)
    u = upper[...]
    inv = invert_upper(u)

    @pl.when(ids[0] == 0)
    def _():
        weight[...] = -inv
        low = u.T
        top[...] = jnp.where(ids[1] == 0, low[:128], low[128:])

    @pl.when(ids[0] != 0)
    def _():
        mine = square(win, 2, 3)
        y = lax.dot_general(
            inv, mine, (((0,), (1,)), ((), ())), precision=precise, preferred_element_type=F32
        )
        weight[...] = jnp.dot(inv, y, precision=precise, preferred_element_type=F32)
        top[...] = jnp.zeros_like(top)


def factor(ids, win):
    vmem = pl.BlockSpec(memory_space=pltpu.VMEM)
    return pl.pallas_call(
        factor_kernel,
        out_shape=[jax.ShapeDtypeStruct((256, 256), F32), jax.ShapeDtypeStruct((128, 256), F32)],
        in_specs=[pl.BlockSpec(memory_space=pltpu.SMEM), vmem],
        out_specs=[vmem, vmem],
        scratch_shapes=[pltpu.VMEM((256, 256), F32)] * 2,
        compiler_params=pltpu.CompilerParams(vmem_limit_bytes=40 << 20),
        name="factor",
    )(ids, win)


def update_kernel(ids, panel, slab, weight, top, out):
    even, odd = pl.ds(0, 512, 2), pl.ds(1, 512, 2)
    keep = (ids[0] != 0).astype(F32)
    a = jnp.concatenate([panel[even, :], panel[odd, :]], axis=1)
    d = jnp.dot(a, weight[...], precision=precise, preferred_element_type=F32)
    out[even, :] = keep * slab[even, :] - d[:, :128]
    out[odd, :] = keep * slab[odd, :] - d[:, 128:]

    @pl.when((pl.program_id(0) == 0) & (ids[1] < 2))
    def _():
        out[pl.ds(0, 128, 2), :] = top[:, :128]
        out[pl.ds(1, 128, 2), :] = top[:, 128:]


def update(ids, panel, slab, weight, top):
    tile = pl.BlockSpec((1024, 128), lambda i: (i, 0))
    whole = pl.BlockSpec((256, 256), lambda i: (0, 0))
    return pl.pallas_call(
        update_kernel,
        grid=(8,),
        out_shape=jax.ShapeDtypeStruct((8192, 128), F32),
        in_specs=[
            pl.BlockSpec(memory_space=pltpu.SMEM),
            tile,
            tile,
            whole,
            pl.BlockSpec((128, 256), lambda i: (0, 0)),
        ],
        out_specs=tile,
        compiler_params=pltpu.CompilerParams(vmem_limit_bytes=40 << 20),
        name="update",
    )(ids, panel, slab, weight, top)


def local(front_slab, child_keep, child_give, map_keep, map_give):
    front_id = lax.axis_index("front")
    row_id = lax.axis_index("row")
    col_id = lax.axis_index("col")
    front = front_slab.reshape(32, 256, 128)
    keep = child_keep.reshape(8, 256, 128)
    give = child_give.reshape(8, 256, 128)
    kept = lax.dynamic_index_in_dim(map_keep, front_id, 0, keepdims=False)
    moved = lax.dynamic_index_in_dim(map_give, front_id ^ 1, 0, keepdims=False)
    tables = jnp.stack([kept.T.reshape(32), moved.T.reshape(32)])
    parent = jnp.arange(32, dtype=jnp.int32) * 4 + row_id
    slot = jnp.arange(64, dtype=jnp.int32).reshape(2, 1, 32)
    hit = tables[:, None, :] == parent[None, :, None]
    inv = (64 + jnp.sum(jnp.where(hit, slot - 64, 0), axis=2)).reshape(64).astype(jnp.int32)
    ids = jnp.stack([col_id, row_id]).astype(jnp.int32)
    panel, slab, win = exchange(inv, front, keep, give)
    weight, top = factor(ids, win)
    out = update(ids, panel.reshape(8192, 128), slab.reshape(8192, 128), weight, top)
    return out.reshape(front_slab.shape)


def solution(mesh):
    spec = P("front", None, "row", None, None, "col", None)
    return jax.shard_map(
        local,
        mesh=mesh,
        in_specs=(spec, spec, spec, P(), P()),
        out_specs=spec,
        check_vma=False,
    )
```

```python
import functools

import jax
import jax.numpy as jnp
from jax import lax
from jax.experimental import pallas as pl
from jax.experimental.pallas import tpu as pltpu
from jax.sharding import PartitionSpec as P

F32 = jnp.float32
BF16 = jnp.bfloat16
precise = lax.Precision.HIGHEST

CHUNKS = (8, 8, 16, 16, 16, 16, 16, 16, 16)
STARTS = tuple(sum(CHUNKS[:i]) for i in range(len(CHUNKS)))
NCH = len(CHUNKS)
WINDOW = 3
TILE = 1024
GROUPS = 4
PARTS = 16 * GROUPS
SKEW = 5
EXTRA = 14 * GROUPS
SLOTS = PARTS + 1
HALF_AT = PARTS // 2 + 6 * SKEW
LEAD_AT = 3
PANELS = {3: (0, 5), 4: (5, 10), 5: (10, 16)}
LEVELS = {6: (0, 4), 7: (4, 8)}
LATE = 2 * GROUPS
BEHIND = 1


def place():
    front = lax.axis_index("front")
    row = lax.axis_index("row")
    col = lax.axis_index("col")
    x = (row // 2) * 2 + front % 2
    return x, front // 2, col, row % 2


def device(x, y, z, core):
    x = lax.rem(x + 4, 4)
    z = lax.rem(z + 8, 8)
    return {"front": y * 2 + x % 2, "row": (x // 2) * 2 + core, "col": z}


def row_of(x, core):
    return (lax.rem(x + 4, 4) // 2) * 2 + core


def exchange_kernel(
    inv,
    front_hbm,
    keep_hbm,
    give_hbm,
    panel_out,
    slab_out,
    window_out,
    inverse_out,
    upper_out,
    slab,
    panel,
    win,
    early,
    mix,
    halves,
    work,
    upper,
    inverse,
    load_sem,
    own_sem,
    xs,
    xr,
    ms,
    mr,
    zs,
    zr,
    ws,
    wr,
    es,
    bs,
    br,
    us,
    ur,
    vs,
    vr,
    out_sem,
    *pools,
):
    x, y, z, core = place()
    row = row_of(x, core)
    mate = device(x, y, z, 1 - core)
    far = device(x + 2, y, z, core)
    far_mate = device(x + 2, y, z, 1 - core)
    up = device(x + 1, y, z, core)
    down = device(x - 1, y, z, core)
    nxt = device(x, y, z + 1, core)
    prv = device(x, y, z - 1, core)
    row_far = lax.rem(row + 2, 4)
    row_mate = row_of(x, 1 - core)
    row_mate_far = lax.rem(row_mate + 2, 4)
    row_up = row_of(x + 1, core)
    row_down = row_of(x - 1, core)
    row_up_mate = row_of(x + 1, 1 - core)
    row_down_mate = row_of(x - 1, 1 - core)

    load = pltpu.make_async_copy(front_hbm, slab, load_sem)
    load.start()

    barrier = pltpu.get_barrier_semaphore()
    for target in (mate, far, far_mate, up, down, nxt, prv):
        pl.semaphore_signal(barrier, 1, device_id=target)
    pl.semaphore_wait(barrier, 7)

    def rows(j):
        return pl.ds(2 * STARTS[j], 2 * CHUNKS[j])

    def eight(base):
        return pl.ds(base, 8)

    def remote(src, dst, s, r, dev):
        return pltpu.make_async_remote_copy(src, dst, s, r, device_id=dev)

    def send_x(j):
        pool = pools[j]
        keep = keep_hbm.at[:, rows(j)]
        give = give_hbm.at[:, rows(j)]
        mine = pool.at[eight(8 * row)]
        given = pool.at[eight(32 + 8 * row)]
        return (
            remote(keep, mine, xs.at[0, j], xr.at[0, j], far),
            remote(give, given, xs.at[1, j], xr.at[1, j], up),
            remote(give, given, xs.at[2, j], xr.at[2, j], down),
        )

    def recv_x(j):
        pool = pools[j]
        give = give_hbm.at[:, rows(j)]
        return (
            remote(give, pool.at[eight(8 * row_far)], xs.at[0, j], xr.at[0, j], far),
            remote(give, pool.at[eight(32 + 8 * row_down)], xs.at[1, j], xr.at[1, j], down),
            remote(give, pool.at[eight(32 + 8 * row_up)], xs.at[2, j], xr.at[2, j], up),
        )

    def own_copy(j):
        return pltpu.make_async_copy(
            keep_hbm.at[:, rows(j)], pools[j].at[eight(8 * row)], own_sem.at[j]
        )

    def own_relay(j):
        mine = pools[j].at[eight(8 * row)]
        return remote(keep_hbm.at[:, rows(j)], mine, ms.at[0, j], mr.at[0, j], mate)

    def relays(j):
        out = []
        for p, base in ((1, 8 * row_far), (2, 32 + 8 * row_down), (3, 32 + 8 * row_up)):
            part = pools[j].at[eight(base)]
            out.append(remote(part, part, ms.at[p, j], mr.at[p, j], mate))
        return out

    def relayed(j):
        out = []
        for p, base in (
            (0, 8 * row_mate),
            (1, 8 * row_mate_far),
            (2, 32 + 8 * row_down_mate),
            (3, 32 + 8 * row_up_mate),
        ):
            part = pools[j].at[eight(base)]
            out.append(remote(part, part, ms.at[p, j], mr.at[p, j], mate))
        return out

    def begin_x(j):
        for c in send_x(j):
            c.start()
        own_copy(j).start()
        own_relay(j).start()

    def arrive_x(j):
        for c in recv_x(j):
            c.wait_recv()
        for c in relays(j):
            c.start()

    def assemble(j):
        own_copy(j).wait()
        for c in relayed(j):
            c.wait_recv()
        pool = pools[j]

        def one(b, carry):
            kept = pool[inv[b]]
            moved = pool[inv[32 + b]]
            slab[b, rows(j), :] = slab[b, rows(j), :] + kept + moved
            return carry

        lax.fori_loop(0, 32, one, 0, unroll=4)

    def part(ref, way, t):
        span = 16 // GROUPS
        base = 16 * way + span * (t % GROUPS)
        return ref.at[pl.ds(base, span), pl.ds(pl.multiple_of(16 * (t // GROUPS), 16), 16)]

    def hop(ref, way, t):
        return remote(
            part(ref, way, t),
            part(panel, way, t),
            zs.at[way, t],
            zr.at[way, t],
            prv if way else nxt,
        )

    def early_copy(i):
        return pltpu.make_async_copy((keep_hbm, give_hbm)[i], early.at[i, pl.ds(0, 8)], es.at[i])

    def swap(i):
        return remote(mix.at[2 * i + 1 - core], mix.at[4 + i], bs.at[i], br.at[i], mate)

    def across(i):
        return remote(
            mix.at[6 + min(i, 1)], mix.at[8 + i], bs.at[2 + i], br.at[2 + i], (far, up, down)[i]
        )

    def trade():
        return remote(halves.at[core], halves.at[core], bs.at[5], br.at[5], mate)

    def trade_in():
        return remote(halves.at[1 - core], halves.at[1 - core], bs.at[5], br.at[5], mate)

    def lead_begin():
        for i in (0, 1):
            early_copy(i).wait()
        for i in (0, 1):
            for p in (0, 1):
                mix[2 * i + p] = early[i, inv[64 + 2 * i + p]]
        for i in (0, 1):
            swap(i).start()
        for i in (0, 1):
            swap(i).wait_recv()
        mine = mix[core] + mix[4]
        mix[6] = jnp.where(row < 2, mine + slab[0], mine)
        mix[7] = mix[2 + core] + mix[5]
        for i in range(3):
            across(i).start()

    def lead_end():
        for i in range(3):
            across(i).wait_recv()
        halves[core] = mix[6] + mix[8] + mix[9] + mix[10]
        trade().start()
        trade_in().wait_recv()
        lead = square(halves, 0, 1)
        work[...] = 0.5 * (lead + lead.T)

    def extra(way):
        ref = inverse.at[pl.ds(pl.multiple_of(128 * core + 64 * way, 64), 64)]
        return remote(ref, ref, us.at[way], ur.at[way], prv if way else nxt)

    def extra_mate(way):
        ref = inverse.at[pl.ds(pl.multiple_of(128 * core + 64 * way, 64), 64)]
        return remote(ref, ref, vs.at[way], vr.at[way], mate)

    def extra_from_mate(way):
        ref = inverse.at[pl.ds(pl.multiple_of(128 * (1 - core) + 64 * way, 64), 64)]
        return remote(ref, ref, vs.at[way], vr.at[way], mate)

    for j in range(NCH):
        pools[j][64] = jnp.zeros(pools[j].shape[1:], F32)
    for j in range(WINDOW):
        begin_x(j)
    load.wait()

    @pl.when(z == 0)
    def _():
        for i in (0, 1):
            early_copy(i).start()
            early[i, 8] = jnp.zeros((256, 128), F32)
        lead_begin()
        for j in range(NCH):
            arrive_x(j)
            if j + WINDOW < NCH:
                begin_x(j + WINDOW)
            assemble(j)

            def launch(t, carry):
                for way in (0, 1):
                    hop(slab, way, t).start()
                return carry

            first = STARTS[j] // 8 * GROUPS
            end = first + CHUNKS[j] // 8 * GROUPS
            lax.fori_loop(first, end, launch, 0)
            if end == EXTRA:
                levels(inverse, upper, *LEVELS[j])
                for way in (0, 1):
                    extra(way).start()
                continue
            if j == LEAD_AT:
                lead_end()
            if j in PANELS:
                for p in range(*PANELS[j]):
                    factor_panel(work, upper, 16 * p)
            if j in LEVELS:
                levels(inverse, upper, *LEVELS[j])

    half = z // 2
    owner = 2 * lax.rem(z, 2)

    def spread(h, k):
        src = panel.at[half, pl.ds(128 * k, 128)]
        dst = win.at[h, pl.ds(128 * k, 128)]
        return [
            remote(src, dst, ws.at[k, i], wr.at[h, k], dev)
            for i, dev in enumerate((mate, far, far_mate))
        ]

    def share(k):
        for h in (0, 1):

            @pl.when(row == owner + h)
            def _():
                for c in spread(h, k):
                    c.start()
                win[h, pl.ds(128 * k, 128), :] = panel[half, pl.ds(128 * k, 128), :]

    @pl.when(z != 0)
    def _():
        total = SLOTS + SKEW * 6

        def step(s, carry):
            for way in (0, 1):
                lag = (7 - z) if way else (z - 1)
                e = s - SKEW * lag
                t = e - (e > EXTRA).astype(jnp.int32)

                def pass_on(copy):
                    copy.wait_recv()

                    @pl.when(lag < 6)
                    def _():
                        copy.start()

                @pl.when((e >= 0) & (e < SLOTS) & (e != EXTRA))
                def _():
                    pass_on(hop(panel, way, t))

                @pl.when(e == EXTRA)
                def _():
                    pass_on(extra(way))
                    extra_mate(way).start()

            return carry

        done = 0
        shared = False
        for j in range(NCH):
            until = (STARTS[j] + CHUNKS[j]) // 8 * GROUPS + LATE
            if until >= HALF_AT and not shared:
                lax.fori_loop(done, HALF_AT, step, 0)
                done = HALF_AT
                share(0)
                shared = True
            lax.fori_loop(done, until, step, 0)
            done = until
            arrive_x(j)
            if j + WINDOW < NCH:
                begin_x(j + WINDOW)
            if j >= BEHIND:
                assemble(j - BEHIND)
        if not shared:
            lax.fori_loop(done, HALF_AT, step, 0)
            done = HALF_AT
            share(0)
        lax.fori_loop(done, total, step, 0)
        share(1)
        for j in range(max(0, NCH - BEHIND), NCH):
            assemble(j)

    pltpu.make_async_copy(slab, slab_out, out_sem.at[1]).start()

    @pl.when(z == 0)
    def _():
        pltpu.make_async_copy(slab, panel_out, out_sem.at[0]).start()
        copy = pltpu.make_async_copy(upper, upper_out, out_sem.at[4])
        copy.start()
        win[...] = jnp.zeros_like(win)
        copy.wait()

    @pl.when(z != 0)
    def _():
        pltpu.make_async_copy(panel, panel_out, out_sem.at[0]).start()
        for way in (0, 1):
            extra_from_mate(way).wait_recv()
        for h in (0, 1):

            @pl.when(row != owner + h)
            def _():
                for k in (0, 1):
                    ref = win.at[h, pl.ds(128 * k, 128)]
                    remote(ref, ref, ws.at[k, 0], wr.at[h, k], mate).wait_recv()

    pltpu.make_async_copy(win, window_out, out_sem.at[2]).start()
    pltpu.make_async_copy(inverse, inverse_out, out_sem.at[3]).start()

    @pl.when(z == 0)
    def _():
        for i in (0, 1):
            swap(i).wait_send()
        for i in range(3):
            across(i).wait_send()
        trade().wait_send()

    @pl.when(z != 0)
    def _():
        for way in (0, 1):
            extra_mate(way).wait_send()
        for h in (0, 1):

            @pl.when(row == owner + h)
            def _():
                for k in (0, 1):
                    for c in spread(h, k):
                        c.wait_send()

    for way in (0, 1):

        @pl.when(z != (1 if way else 7))
        def _():
            extra(way).wait_send()

    for j in range(NCH):
        for c in send_x(j):
            c.wait_send()
        own_relay(j).wait_send()
        for c in relays(j):
            c.wait_send()

    def drain(t, carry):
        for way in (0, 1):
            last = 1 if way else 7

            @pl.when(z != last)
            def _():
                hop(panel, way, t).wait_send()

        return carry

    lax.fori_loop(0, PARTS, drain, 0)
    pltpu.make_async_copy(panel, panel_out, out_sem.at[0]).wait()
    pltpu.make_async_copy(slab, slab_out, out_sem.at[1]).wait()
    pltpu.make_async_copy(win, window_out, out_sem.at[2]).wait()
    pltpu.make_async_copy(inverse, inverse_out, out_sem.at[3]).wait()


def exchange(inv, front, keep, give):
    big = jax.ShapeDtypeStruct(front.shape, F32)
    square_shape = jax.ShapeDtypeStruct((256, 256), F32)
    anywhere = pl.BlockSpec(memory_space=pl.ANY)
    dma = pltpu.SemaphoreType.DMA
    return pl.pallas_call(
        exchange_kernel,
        out_shape=[big, big, jax.ShapeDtypeStruct((2, 256, 128), F32), square_shape, square_shape],
        in_specs=[pl.BlockSpec(memory_space=pltpu.SMEM)] + [anywhere] * 3,
        out_specs=[anywhere] * 5,
        scratch_shapes=[
            pltpu.VMEM(front.shape, F32),
            pltpu.VMEM(front.shape, F32),
            pltpu.VMEM((2, 256, 128), F32),
            pltpu.VMEM((2, 9, 256, 128), F32),
            pltpu.VMEM((11, 256, 128), F32),
            pltpu.VMEM((2, 256, 128), F32),
            pltpu.VMEM((256, 256), F32),
            pltpu.VMEM((256, 256), F32),
            pltpu.VMEM((256, 256), F32),
            dma,
            dma((NCH,)),
            dma((3, NCH)),
            dma((3, NCH)),
            dma((4, NCH)),
            dma((4, NCH)),
            dma((2, PARTS)),
            dma((2, PARTS)),
            dma((2, 3)),
            dma((2, 2)),
            dma((2,)),
            dma((6,)),
            dma((6,)),
            dma((2,)),
            dma((2,)),
            dma((2,)),
            dma((2,)),
            dma((5,)),
        ]
        + [pltpu.VMEM((65, 2 * n, 128), F32) for n in CHUNKS],
        compiler_params=pltpu.CompilerParams(
            collective_id=0, has_side_effects=True, vmem_limit_bytes=40 << 20
        ),
        name="exchange",
    )(inv, front, keep, give)


def three(a):
    hi = a.astype(BF16)
    rest = a - hi.astype(F32)
    mid = rest.astype(BF16)
    low = (rest - mid.astype(F32)).astype(BF16)
    return hi, mid, low


def factor_panel(work, upper, j0, n=16):
    r = work[j0 : j0 + n, :]
    sub = lax.broadcasted_iota(jnp.int32, (n, 128), 0)
    sub2 = lax.broadcasted_iota(jnp.int32, (n, 256), 0)
    lane2 = lax.broadcasted_iota(jnp.int32, (n, 256), 1)
    g = [jnp.broadcast_to(r[:, j0 + i : j0 + i + 1], (n, 128)) for i in range(n)]
    for i in range(n):
        inv = lax.rsqrt(g[i][i : i + 1, :])
        l = g[i] * inv
        below = jnp.where(sub > i, l, 0.0)
        for m in range(i + 1, n):
            g[m] = g[m] - below * l[m : m + 1, :]
        line = r[i : i + 1, :] * jnp.concatenate([inv, inv], axis=1)
        r = jnp.where(sub2 == i, line, r - jnp.concatenate([below, below], axis=1) * line)
    r = jnp.where(lane2 >= sub2 + j0, r, 0.0)
    upper[j0 : j0 + n, :] = r
    if j0 + n < 256:
        h, m, l = three(r)
        a = jnp.concatenate([h, h, m, h, l, m], axis=0)
        b = jnp.concatenate([h, m, h, l, h, m], axis=0)
        t = lax.dot_general(a, b, (((0,), (0,)), ((), ())), preferred_element_type=F32)
        work[j0 + n :, :] = work[j0 + n :, :] - t[j0 + n :, :]


def levels(inverse, upper, first, end):
    i = lax.broadcasted_iota(jnp.int32, (256, 256), 0)
    j = lax.broadcasted_iota(jnp.int32, (256, 256), 1)
    u = upper[...]
    if first == 0:
        inv = jnp.where(i == j, 1.0 / jnp.where(i == j, u, 1.0), 0.0)
    else:
        inv = inverse[...]
    for level in range(first, end):
        s = 1 << level
        off = jnp.where((i // (2 * s) == j // (2 * s)) & (i // s < j // s), u, 0.0)
        step = jnp.dot(inv, off, precision=precise, preferred_element_type=F32)
        inv = inv - jnp.dot(step, inv, precision=precise, preferred_element_type=F32)
    inverse[...] = inv


def square(ref, a, b):
    even, odd = pl.ds(0, 128, 2), pl.ds(1, 128, 2)
    top = jnp.concatenate([ref[a, even, :], ref[a, odd, :]], axis=1)
    low = jnp.concatenate([ref[b, even, :], ref[b, odd, :]], axis=1)
    return jnp.concatenate([top, low], axis=0)


def update_kernel(ids, panel, slab, win, inverse, upper, out, weight, top):
    even, odd = pl.ds(0, TILE, 2), pl.ds(1, TILE, 2)

    @pl.when(pl.program_id(0) == 0)
    def _():
        inv = inverse[...]

        @pl.when(ids[0] == 0)
        def _():
            weight[...] = -inv
            low = upper[...].T
            top[...] = jnp.where(ids[1] == 0, low[:128], low[128:])

        @pl.when(ids[0] != 0)
        def _():
            y = lax.dot_general(
                inv,
                square(win, 0, 1),
                (((0,), (1,)), ((), ())),
                precision=precise,
                preferred_element_type=F32,
            )
            weight[...] = jnp.dot(inv, y, precision=precise, preferred_element_type=F32)
            top[...] = jnp.zeros_like(top)

    keep = (ids[0] != 0).astype(F32)
    a = jnp.concatenate([panel[even, :], panel[odd, :]], axis=1)
    d = jnp.dot(a, weight[...], precision=precise, preferred_element_type=F32)
    out[even, :] = keep * slab[even, :] - d[:, :128]
    out[odd, :] = keep * slab[odd, :] - d[:, 128:]

    @pl.when((pl.program_id(0) == 0) & (ids[1] < 2))
    def _():
        out[pl.ds(0, 128, 2), :] = top[:, :128]
        out[pl.ds(1, 128, 2), :] = top[:, 128:]


def update(ids, panel, slab, win, inverse, upper):
    tile = pl.BlockSpec((2 * TILE, 128), lambda i: (i, 0))
    whole = pl.BlockSpec((256, 256), lambda i: (0, 0))
    return pl.pallas_call(
        update_kernel,
        grid=(4096 // TILE,),
        out_shape=jax.ShapeDtypeStruct((8192, 128), F32),
        in_specs=[
            pl.BlockSpec(memory_space=pltpu.SMEM),
            tile,
            tile,
            pl.BlockSpec((2, 256, 128), lambda i: (0, 0, 0)),
            whole,
            whole,
        ],
        out_specs=tile,
        scratch_shapes=[pltpu.VMEM((256, 256), F32), pltpu.VMEM((128, 256), F32)],
        compiler_params=pltpu.CompilerParams(vmem_limit_bytes=40 << 20),
        name="update",
    )(ids, panel, slab, win, inverse, upper)


def local(front_slab, child_keep, child_give, map_keep, map_give):
    front_id = lax.axis_index("front")
    row_id = lax.axis_index("row")
    col_id = lax.axis_index("col")
    front = front_slab.reshape(32, 256, 128)
    keep = child_keep.reshape(8, 256, 128)
    give = child_give.reshape(8, 256, 128)
    kept = lax.dynamic_index_in_dim(map_keep, front_id, 0, keepdims=False)
    moved = lax.dynamic_index_in_dim(map_give, front_id ^ 1, 0, keepdims=False)
    tables = jnp.stack([kept.T.reshape(32), moved.T.reshape(32)])
    parent = jnp.arange(32, dtype=jnp.int32) * 4 + row_id
    slot = jnp.arange(64, dtype=jnp.int32).reshape(2, 1, 32)
    hit = tables[:, None, :] == parent[None, :, None]
    inv = (64 + jnp.sum(jnp.where(hit, slot - 64, 0), axis=2)).reshape(64).astype(jnp.int32)
    ids = jnp.stack([col_id, row_id]).astype(jnp.int32)
    given = lax.dynamic_index_in_dim(map_give, front_id, 0, keepdims=False)
    mine = lax.dynamic_index_in_dim(jnp.stack([kept, given]), row_id, 2, keepdims=False)
    own = jnp.arange(8, dtype=jnp.int32)
    lead = mine[:, None, :] == jnp.arange(2, dtype=jnp.int32)[None, :, None]
    lead = (8 + jnp.sum(jnp.where(lead, own - 8, 0), axis=2)).reshape(4).astype(jnp.int32)
    inv = jnp.concatenate([inv, lead])
    panel, slab, win, inverse, upper = exchange(inv, front, keep, give)
    out = update(ids, panel.reshape(8192, 128), slab.reshape(8192, 128), win, inverse, upper)
    return out.reshape(front_slab.shape)


def solution(mesh):
    spec = P("front", None, "row", None, None, "col", None)
    return jax.shard_map(
        local,
        mesh=mesh,
        in_specs=(spec, spec, spec, P(), P()),
        out_specs=spec,
        check_vma=False,
    )
```

```python
import functools

import jax
import jax.numpy as jnp
from jax import lax
from jax.experimental import pallas as pl
from jax.experimental.pallas import tpu as pltpu
from jax.sharding import PartitionSpec as P

F32 = jnp.float32
BF16 = jnp.bfloat16
precise = lax.Precision.HIGHEST

CHUNKS = (8, 8, 16, 16, 16, 16, 16, 16, 8, 8)
STARTS = tuple(sum(CHUNKS[:i]) for i in range(len(CHUNKS)))
NCH = len(CHUNKS)
WINDOW = 3
TILE = 1024
GROUPS = 4
PARTS = 16 * GROUPS
SKEW = 5
ROUND = 14 * GROUPS
BOTH = 2 * (PARTS - ROUND)
SLOTS = ROUND + 2 + BOTH
CUT = 96
CUT_AT = CUT // 8 * GROUPS + 6 * SKEW
LEAD_AT = 3
PANELS = {3: (0, 5), 4: (5, 10), 5: (10, 16)}
LEVELS = {6: (0, 4), 7: (4, 8)}
LATE = 2 * GROUPS
BEHIND = 1


def place():
    front = lax.axis_index("front")
    row = lax.axis_index("row")
    col = lax.axis_index("col")
    x = (row // 2) * 2 + front % 2
    return x, front // 2, col, row % 2


def device(x, y, z, core):
    x = lax.rem(x + 4, 4)
    z = lax.rem(z + 8, 8)
    return {"front": y * 2 + x % 2, "row": (x // 2) * 2 + core, "col": z}


def row_of(x, core):
    return (lax.rem(x + 4, 4) // 2) * 2 + core


def exchange_kernel(
    inv,
    front_hbm,
    keep_hbm,
    give_hbm,
    panel_out,
    slab_out,
    window_out,
    inverse_out,
    upper_out,
    slab,
    panel,
    win,
    early,
    mix,
    halves,
    work,
    upper,
    inverse,
    load_sem,
    own_sem,
    xs,
    xr,
    ms,
    mr,
    zs,
    zr,
    ws,
    wr,
    es,
    bs,
    br,
    us,
    ur,
    vs,
    vr,
    ds,
    dr,
    out_sem,
    row_sem,
    *pools,
):
    x, y, z, core = place()
    row = row_of(x, core)
    mate = device(x, y, z, 1 - core)
    far = device(x + 2, y, z, core)
    far_mate = device(x + 2, y, z, 1 - core)
    up = device(x + 1, y, z, core)
    down = device(x - 1, y, z, core)
    nxt = device(x, y, z + 1, core)
    prv = device(x, y, z - 1, core)
    row_far = lax.rem(row + 2, 4)
    row_mate = row_of(x, 1 - core)
    row_mate_far = lax.rem(row_mate + 2, 4)
    row_up = row_of(x + 1, core)
    row_down = row_of(x - 1, core)
    row_up_mate = row_of(x + 1, 1 - core)
    row_down_mate = row_of(x - 1, 1 - core)

    load = pltpu.make_async_copy(front_hbm, slab, load_sem)
    load.start()

    barrier = pltpu.get_barrier_semaphore()
    for target in (mate, far, far_mate, up, down, nxt, prv):
        pl.semaphore_signal(barrier, 1, device_id=target)
    pl.semaphore_wait(barrier, 7)

    def rows(j):
        return pl.ds(2 * STARTS[j], 2 * CHUNKS[j])

    def eight(base):
        return pl.ds(base, 8)

    def remote(src, dst, s, r, dev):
        return pltpu.make_async_remote_copy(src, dst, s, r, device_id=dev)

    def send_x(j):
        pool = pools[j]
        keep = keep_hbm.at[:, rows(j)]
        give = give_hbm.at[:, rows(j)]
        mine = pool.at[eight(8 * row)]
        given = pool.at[eight(32 + 8 * row)]
        return (
            remote(keep, mine, xs.at[0, j], xr.at[0, j], far),
            remote(give, given, xs.at[1, j], xr.at[1, j], up),
            remote(give, given, xs.at[2, j], xr.at[2, j], down),
        )

    def recv_x(j):
        pool = pools[j]
        give = give_hbm.at[:, rows(j)]
        return (
            remote(give, pool.at[eight(8 * row_far)], xs.at[0, j], xr.at[0, j], far),
            remote(give, pool.at[eight(32 + 8 * row_down)], xs.at[1, j], xr.at[1, j], down),
            remote(give, pool.at[eight(32 + 8 * row_up)], xs.at[2, j], xr.at[2, j], up),
        )

    def own_copy(j):
        return pltpu.make_async_copy(
            keep_hbm.at[:, rows(j)], pools[j].at[eight(8 * row)], own_sem.at[j]
        )

    def own_relay(j):
        mine = pools[j].at[eight(8 * row)]
        return remote(keep_hbm.at[:, rows(j)], mine, ms.at[0, j], mr.at[0, j], mate)

    def relays(j):
        out = []
        for p, base in ((1, 8 * row_far), (2, 32 + 8 * row_down), (3, 32 + 8 * row_up)):
            part = pools[j].at[eight(base)]
            out.append(remote(part, part, ms.at[p, j], mr.at[p, j], mate))
        return out

    def relayed(j):
        out = []
        for p, base in (
            (0, 8 * row_mate),
            (1, 8 * row_mate_far),
            (2, 32 + 8 * row_down_mate),
            (3, 32 + 8 * row_up_mate),
        ):
            part = pools[j].at[eight(base)]
            out.append(remote(part, part, ms.at[p, j], mr.at[p, j], mate))
        return out

    def begin_x(j):
        for c in send_x(j):
            c.start()
        own_copy(j).start()
        own_relay(j).start()

    def arrive_x(j):
        for c in recv_x(j):
            c.wait_recv()
        for c in relays(j):
            c.start()

    def assemble(j):
        own_copy(j).wait()
        for c in relayed(j):
            c.wait_recv()
        pool = pools[j]

        def one(b, carry):
            kept = pool[inv[b]]
            moved = pool[inv[32 + b]]
            slab[b, rows(j), :] = slab[b, rows(j), :] + kept + moved
            return carry

        lax.fori_loop(0, 32, one, 0, unroll=4)

    def part(ref, way, t):
        span = 16 // GROUPS
        base = 16 * way + span * (t % GROUPS)
        return ref.at[pl.ds(base, span), pl.ds(pl.multiple_of(16 * (t // GROUPS), 16), 16)]

    def hop(ref, way, t):
        return remote(
            part(ref, way, t),
            part(panel, way, t),
            zs.at[way, t],
            zr.at[way, t],
            prv if way else nxt,
        )

    def early_copy(i):
        return pltpu.make_async_copy((keep_hbm, give_hbm)[i], early.at[i, pl.ds(0, 8)], es.at[i])

    def swap(i):
        return remote(mix.at[2 * i + 1 - core], mix.at[4 + i], bs.at[i], br.at[i], mate)

    def across(i):
        return remote(
            mix.at[6 + min(i, 1)], mix.at[8 + i], bs.at[2 + i], br.at[2 + i], (far, up, down)[i]
        )

    def trade():
        return remote(halves.at[core], halves.at[core], bs.at[5], br.at[5], mate)

    def trade_in():
        return remote(halves.at[1 - core], halves.at[1 - core], bs.at[5], br.at[5], mate)

    def lead_begin():
        for i in (0, 1):
            early_copy(i).wait()
        for i in (0, 1):
            for p in (0, 1):
                mix[2 * i + p] = early[i, inv[64 + 2 * i + p]]
        for i in (0, 1):
            swap(i).start()
        for i in (0, 1):
            swap(i).wait_recv()
        mine = mix[core] + mix[4]
        mix[6] = jnp.where(row < 2, mine + slab[0], mine)
        mix[7] = mix[2 + core] + mix[5]
        for i in range(3):
            across(i).start()

    def lead_end():
        for i in range(3):
            across(i).wait_recv()
        halves[core] = mix[6] + mix[8] + mix[9] + mix[10]
        trade().start()
        trade_in().wait_recv()
        lead = square(halves, 0, 1)
        work[...] = 0.5 * (lead + lead.T)

    def quarter(c, q):
        return inverse.at[pl.ds(pl.multiple_of(128 * c + 64 * q, 64), 64)]

    def extra(way, q):
        ref = quarter(core, q)
        return remote(ref, ref, us.at[way, q], ur.at[q], prv if way else nxt)

    def extra_mate(q):
        ref = quarter(core, q)
        return remote(ref, ref, vs.at[q], vr.at[q], mate)

    def extra_from_mate(q):
        ref = quarter(1 - core, q)
        return remote(ref, ref, vs.at[q], vr.at[q], mate)

    def both_part(ref, d):
        span = 16 // GROUPS
        row8 = ROUND // GROUPS + d // (2 * GROUPS)
        return ref.at[
            pl.ds(span * (d % (2 * GROUPS)), span), pl.ds(pl.multiple_of(16 * row8, 16), 16)
        ]

    def both(ref, way, d):
        return remote(
            both_part(ref, d), both_part(panel, d), ds.at[way, d], dr.at[d], prv if way else nxt
        )

    def row_copy(j, dst):
        return pltpu.make_async_copy(slab.at[:, rows(j)], dst.at[:, rows(j)], row_sem.at[j])

    for j in range(NCH):
        pools[j][64] = jnp.zeros(pools[j].shape[1:], F32)
    for j in range(WINDOW):
        begin_x(j)
    load.wait()

    @pl.when(z == 0)
    def _():
        for i in (0, 1):
            early_copy(i).start()
            early[i, 8] = jnp.zeros((256, 128), F32)
        lead_begin()
        for j in range(NCH):
            arrive_x(j)
            if j + WINDOW < NCH:
                begin_x(j + WINDOW)
            assemble(j)
            row_copy(j, panel_out).start()

            def launch(t, carry):
                for way in (0, 1):
                    hop(slab, way, t).start()
                return carry

            def launch_both(d, carry):
                for way in (0, 1):
                    both(slab, way, d).start()
                return carry

            first = STARTS[j] // 8 * GROUPS
            end = first + CHUNKS[j] // 8 * GROUPS
            if end <= ROUND:
                lax.fori_loop(first, end, launch, 0)
            else:
                lax.fori_loop(2 * (first - ROUND), 2 * (end - ROUND), launch_both, 0)
            if end == ROUND:
                levels(inverse, upper, *LEVELS[j])
                for way in (0, 1):
                    for q in (0, 1):
                        extra(way, q).start()
                continue
            if j == LEAD_AT:
                lead_end()
            if j in PANELS:
                for p in range(*PANELS[j]):
                    factor_panel(work, upper, 16 * p)
            if j in LEVELS:
                levels(inverse, upper, *LEVELS[j])

    half = z // 2
    owner = 2 * lax.rem(z, 2)

    def cut(k):
        return pl.ds(0, 2 * CUT) if k == 0 else pl.ds(2 * CUT, 256 - 2 * CUT)

    def spread(h, k):
        src = panel.at[half, cut(k)]
        dst = win.at[h, cut(k)]
        return [
            remote(src, dst, ws.at[k, i], wr.at[h, k], dev)
            for i, dev in enumerate((mate, far, far_mate))
        ]

    def panel_copy(k):
        return pltpu.make_async_copy(
            panel.at[:, cut(k)], panel_out.at[:, cut(k)], out_sem.at[k]
        )

    def share(k):
        for h in (0, 1):

            @pl.when(row == owner + h)
            def _():
                for c in spread(h, k):
                    c.start()
                win[h, cut(k), :] = panel[half, cut(k), :]

        panel_copy(k).start()

    @pl.when(z != 0)
    def _():
        total = max(SLOTS + SKEW * 3, ROUND + SKEW * 6)

        def step(s, carry):
            for way in (0, 1):
                lag = (7 - z) if way else (z - 1)
                near = (z > 4) if way else (z <= 4)
                end = 5 if way else 4
                t = s - SKEW * lag

                @pl.when((t >= 0) & (t < ROUND))
                def _():
                    copy = hop(panel, way, t)
                    copy.wait_recv()

                    @pl.when(lag < 6)
                    def _():
                        copy.start()

                @pl.when(near & (t >= ROUND) & (t < SLOTS))
                def _():
                    for q in (0, 1):

                        @pl.when(t == ROUND + q)
                        def _():
                            copy = extra(way, q)
                            copy.wait_recv()

                            @pl.when(z != end)
                            def _():
                                copy.start()

                            extra_mate(q).start()

                    @pl.when(t >= ROUND + 2)
                    def _():
                        copy = both(panel, way, t - ROUND - 2)
                        copy.wait_recv()

                        @pl.when(z != end)
                        def _():
                            copy.start()

            return carry

        done = 0
        shared = False
        for j in range(NCH):
            until = (STARTS[j] + CHUNKS[j]) // 8 * GROUPS + LATE
            if until >= CUT_AT and not shared:
                lax.fori_loop(done, CUT_AT, step, 0)
                done = CUT_AT
                share(0)
                shared = True
            lax.fori_loop(done, until, step, 0)
            done = until
            arrive_x(j)
            if j + WINDOW < NCH:
                begin_x(j + WINDOW)
            if j >= BEHIND:
                assemble(j - BEHIND)
                row_copy(j - BEHIND, slab_out).start()
        if not shared:
            lax.fori_loop(done, CUT_AT, step, 0)
            done = CUT_AT
            share(0)
        lax.fori_loop(done, total, step, 0)
        share(1)
        for j in range(max(0, NCH - BEHIND), NCH):
            assemble(j)
            row_copy(j, slab_out).start()

    @pl.when(z == 0)
    def _():
        copy = pltpu.make_async_copy(upper, upper_out, out_sem.at[4])
        copy.start()
        win[...] = jnp.zeros_like(win)
        copy.wait()

    @pl.when(z != 0)
    def _():
        for q in (0, 1):
            extra_from_mate(q).wait_recv()
        for h in (0, 1):

            @pl.when(row != owner + h)
            def _():
                for k in (0, 1):
                    ref = win.at[h, cut(k)]
                    remote(ref, ref, ws.at[k, 0], wr.at[h, k], mate).wait_recv()

    pltpu.make_async_copy(win, window_out, out_sem.at[2]).start()
    pltpu.make_async_copy(inverse, inverse_out, out_sem.at[3]).start()

    @pl.when(z == 0)
    def _():
        for i in (0, 1):
            swap(i).wait_send()
        for i in range(3):
            across(i).wait_send()
        trade().wait_send()

    @pl.when(z != 0)
    def _():
        for q in (0, 1):
            extra_mate(q).wait_send()
        for k in (0, 1):
            panel_copy(k).wait()
        for h in (0, 1):

            @pl.when(row == owner + h)
            def _():
                for k in (0, 1):
                    for c in spread(h, k):
                        c.wait_send()

    for way in (0, 1):

        @pl.when(((z == 0) | (z > 5)) if way else (z < 4))
        def _():
            for q in (0, 1):
                extra(way, q).wait_send()

            def drain_both(d, carry):
                both(panel, way, d).wait_send()
                return carry

            lax.fori_loop(0, BOTH, drain_both, 0)

    for j in range(NCH):
        for c in send_x(j):
            c.wait_send()
        own_relay(j).wait_send()
        for c in relays(j):
            c.wait_send()

    def drain(t, carry):
        for way in (0, 1):
            last = 1 if way else 7

            @pl.when(z != last)
            def _():
                hop(panel, way, t).wait_send()

        return carry

    lax.fori_loop(0, ROUND, drain, 0)
    for j in range(NCH):
        row_copy(j, slab_out).wait()
    pltpu.make_async_copy(win, window_out, out_sem.at[2]).wait()
    pltpu.make_async_copy(inverse, inverse_out, out_sem.at[3]).wait()


def exchange(inv, front, keep, give):
    big = jax.ShapeDtypeStruct(front.shape, F32)
    square_shape = jax.ShapeDtypeStruct((256, 256), F32)
    anywhere = pl.BlockSpec(memory_space=pl.ANY)
    dma = pltpu.SemaphoreType.DMA
    return pl.pallas_call(
        exchange_kernel,
        out_shape=[big, big, jax.ShapeDtypeStruct((2, 256, 128), F32), square_shape, square_shape],
        in_specs=[pl.BlockSpec(memory_space=pltpu.SMEM)] + [pl.BlockSpec(memory_space=pltpu.HBM)] * 3,
        out_specs=[anywhere] * 5,
        scratch_shapes=[
            pltpu.VMEM(front.shape, F32),
            pltpu.VMEM(front.shape, F32),
            pltpu.VMEM((2, 256, 128), F32),
            pltpu.VMEM((2, 9, 256, 128), F32),
            pltpu.VMEM((11, 256, 128), F32),
            pltpu.VMEM((2, 256, 128), F32),
            pltpu.VMEM((256, 256), F32),
            pltpu.VMEM((256, 256), F32),
            pltpu.VMEM((256, 256), F32),
            dma,
            dma((NCH,)),
            dma((3, NCH)),
            dma((3, NCH)),
            dma((4, NCH)),
            dma((4, NCH)),
            dma((2, ROUND)),
            dma((2, ROUND)),
            dma((2, 3)),
            dma((2, 2)),
            dma((2,)),
            dma((6,)),
            dma((6,)),
            dma((2, 2)),
            dma((2,)),
            dma((2,)),
            dma((2,)),
            dma((2, BOTH)),
            dma((BOTH,)),
            dma((5,)),
            dma((NCH,)),
        ]
        + [pltpu.VMEM((65, 2 * n, 128), F32) for n in CHUNKS],
        compiler_params=pltpu.CompilerParams(
            collective_id=0, has_side_effects=True, vmem_limit_bytes=40 << 20
        ),
        name="exchange",
    )(inv, front, keep, give)


def three(a):
    hi = a.astype(BF16)
    rest = a - hi.astype(F32)
    mid = rest.astype(BF16)
    low = (rest - mid.astype(F32)).astype(BF16)
    return hi, mid, low


def factor_panel(work, upper, j0, n=16):
    r = work[j0 : j0 + n, :]
    sub = lax.broadcasted_iota(jnp.int32, (n, 128), 0)
    sub2 = lax.broadcasted_iota(jnp.int32, (n, 256), 0)
    lane2 = lax.broadcasted_iota(jnp.int32, (n, 256), 1)
    g = [jnp.broadcast_to(r[:, j0 + i : j0 + i + 1], (n, 128)) for i in range(n)]
    for i in range(n):
        inv = lax.rsqrt(g[i][i : i + 1, :])
        l = g[i] * inv
        below = jnp.where(sub > i, l, 0.0)
        for m in range(i + 1, n):
            g[m] = g[m] - below * l[m : m + 1, :]
        line = r[i : i + 1, :] * jnp.concatenate([inv, inv], axis=1)
        r = jnp.where(sub2 == i, line, r - jnp.concatenate([below, below], axis=1) * line)
    r = jnp.where(lane2 >= sub2 + j0, r, 0.0)
    upper[j0 : j0 + n, :] = r
    if j0 + n < 256:
        h, m, l = three(r)
        a = jnp.concatenate([h, h, m, h, l, m], axis=0)
        b = jnp.concatenate([h, m, h, l, h, m], axis=0)
        t = lax.dot_general(a, b, (((0,), (0,)), ((), ())), preferred_element_type=F32)
        work[j0 + n :, :] = work[j0 + n :, :] - t[j0 + n :, :]


def levels(inverse, upper, first, end):
    i = lax.broadcasted_iota(jnp.int32, (256, 256), 0)
    j = lax.broadcasted_iota(jnp.int32, (256, 256), 1)
    u = upper[...]
    if first == 0:
        inv = jnp.where(i == j, 1.0 / jnp.where(i == j, u, 1.0), 0.0)
    else:
        inv = inverse[...]
    for level in range(first, end):
        s = 1 << level
        off = jnp.where((i // (2 * s) == j // (2 * s)) & (i // s < j // s), u, 0.0)
        step = jnp.dot(inv, off, precision=precise, preferred_element_type=F32)
        inv = inv - jnp.dot(step, inv, precision=precise, preferred_element_type=F32)
    inverse[...] = inv


def square(ref, a, b):
    even, odd = pl.ds(0, 128, 2), pl.ds(1, 128, 2)
    top = jnp.concatenate([ref[a, even, :], ref[a, odd, :]], axis=1)
    low = jnp.concatenate([ref[b, even, :], ref[b, odd, :]], axis=1)
    return jnp.concatenate([top, low], axis=0)


def update_kernel(ids, panel, slab, win, inverse, upper, out, weight, top):
    even, odd = pl.ds(0, TILE, 2), pl.ds(1, TILE, 2)

    @pl.when(pl.program_id(0) == 0)
    def _():
        inv = inverse[...]

        @pl.when(ids[0] == 0)
        def _():
            weight[...] = -inv
            low = upper[...].T
            top[...] = jnp.where(ids[1] == 0, low[:128], low[128:])

        @pl.when(ids[0] != 0)
        def _():
            y = lax.dot_general(
                inv,
                square(win, 0, 1),
                (((0,), (1,)), ((), ())),
                precision=precise,
                preferred_element_type=F32,
            )
            weight[...] = jnp.dot(inv, y, precision=precise, preferred_element_type=F32)
            top[...] = jnp.zeros_like(top)

    a = jnp.concatenate([panel[even, :], panel[odd, :]], axis=1)
    d = jnp.dot(a, weight[...], precision=precise, preferred_element_type=F32)
    out[even, :] = jnp.where(ids[0] != 0, slab[even, :], 0.0) - d[:, :128]
    out[odd, :] = jnp.where(ids[0] != 0, slab[odd, :], 0.0) - d[:, 128:]

    @pl.when((pl.program_id(0) == 0) & (ids[1] < 2))
    def _():
        out[pl.ds(0, 128, 2), :] = top[:, :128]
        out[pl.ds(1, 128, 2), :] = top[:, 128:]


def update(ids, panel, slab, win, inverse, upper):
    tile = pl.BlockSpec((2 * TILE, 128), lambda i: (i, 0))
    whole = pl.BlockSpec((256, 256), lambda i: (0, 0))
    return pl.pallas_call(
        update_kernel,
        grid=(4096 // TILE,),
        out_shape=jax.ShapeDtypeStruct((8192, 128), F32),
        in_specs=[
            pl.BlockSpec(memory_space=pltpu.SMEM),
            tile,
            tile,
            pl.BlockSpec((2, 256, 128), lambda i: (0, 0, 0)),
            whole,
            whole,
        ],
        out_specs=tile,
        scratch_shapes=[pltpu.VMEM((256, 256), F32), pltpu.VMEM((128, 256), F32)],
        compiler_params=pltpu.CompilerParams(vmem_limit_bytes=40 << 20),
        name="update",
    )(ids, panel, slab, win, inverse, upper)


def local(front_slab, child_keep, child_give, map_keep, map_give):
    front_id = lax.axis_index("front")
    row_id = lax.axis_index("row")
    col_id = lax.axis_index("col")
    front, keep, give = (
        pltpu.with_memory_space_constraint(a.reshape(n, 256, 128), pltpu.HBM)
        for a, n in ((front_slab, 32), (child_keep, 8), (child_give, 8))
    )
    kept = lax.dynamic_index_in_dim(map_keep, front_id, 0, keepdims=False)
    moved = lax.dynamic_index_in_dim(map_give, front_id ^ 1, 0, keepdims=False)
    tables = jnp.stack([kept.T.reshape(32), moved.T.reshape(32)])
    parent = jnp.arange(32, dtype=jnp.int32) * 4 + row_id
    slot = jnp.arange(64, dtype=jnp.int32).reshape(2, 1, 32)
    hit = tables[:, None, :] == parent[None, :, None]
    inv = (64 + jnp.sum(jnp.where(hit, slot - 64, 0), axis=2)).reshape(64).astype(jnp.int32)
    ids = jnp.stack([col_id, row_id]).astype(jnp.int32)
    given = lax.dynamic_index_in_dim(map_give, front_id, 0, keepdims=False)
    mine = lax.dynamic_index_in_dim(jnp.stack([kept, given]), row_id, 2, keepdims=False)
    own = jnp.arange(8, dtype=jnp.int32)
    lead = mine[:, None, :] == jnp.arange(2, dtype=jnp.int32)[None, :, None]
    lead = (8 + jnp.sum(jnp.where(lead, own - 8, 0), axis=2)).reshape(4).astype(jnp.int32)
    inv = jnp.concatenate([inv, lead])
    panel, slab, win, inverse, upper = exchange(inv, front, keep, give)
    out = update(ids, panel.reshape(8192, 128), slab.reshape(8192, 128), win, inverse, upper)
    return out.reshape(front_slab.shape)


def solution(mesh):
    spec = P("front", None, "row", None, None, "col", None)
    return jax.shard_map(
        local,
        mesh=mesh,
        in_specs=(spec, spec, spec, P(), P()),
        out_specs=spec,
        check_vma=False,
    )
```

```python
import functools

import jax
import jax.numpy as jnp
from jax import lax
from jax.experimental import pallas as pl
from jax.experimental.pallas import tpu as pltpu
from jax.sharding import PartitionSpec as P

F32 = jnp.float32
BF16 = jnp.bfloat16
precise = lax.Precision.HIGHEST

CHUNKS = (8, 8, 16, 16, 16, 16, 16, 16, 8, 8)
STARTS = tuple(sum(CHUNKS[:i]) for i in range(len(CHUNKS)))
NCH = len(CHUNKS)
WINDOW = 3
TILE = 1024
GROUPS = 4
PARTS = 16 * GROUPS
SKEW = 5
ROUND = 14 * GROUPS
BOTH = 2 * (PARTS - ROUND)
SLOTS = ROUND + 2 + BOTH
CUT = 96
CUT_AT = CUT // 8 * GROUPS + 6 * SKEW
LEAD_AT = 4
LEAD_STEP = 12
PANELS = {4: (0, 5), 5: (5, 10), 6: (10, 16)}
LEVELS = {7: (0, 8)}
LATE = 2 * GROUPS
BEHIND = 1


def place():
    front = lax.axis_index("front")
    row = lax.axis_index("row")
    col = lax.axis_index("col")
    x = (row // 2) * 2 + front % 2
    return x, front // 2, col, row % 2


def device(x, y, z, core):
    x = lax.rem(x + 4, 4)
    z = lax.rem(z + 8, 8)
    return {"front": y * 2 + x % 2, "row": (x // 2) * 2 + core, "col": z}


def row_of(x, core):
    return (lax.rem(x + 4, 4) // 2) * 2 + core


def exchange_kernel(
    inv,
    front_hbm,
    keep_hbm,
    give_hbm,
    panel_out,
    slab_out,
    window_out,
    inverse_out,
    upper_out,
    slab,
    panel,
    win,
    early,
    mix,
    halves,
    work,
    upper,
    inverse,
    load_sem,
    own_sem,
    xs,
    xr,
    ms,
    mr,
    zs,
    zr,
    ws,
    wr,
    es,
    bs,
    br,
    us,
    ur,
    vs,
    vr,
    ds,
    dr,
    out_sem,
    row_sem,
    *pools,
):
    x, y, z, core = place()
    row = row_of(x, core)
    mate = device(x, y, z, 1 - core)
    far = device(x + 2, y, z, core)
    far_mate = device(x + 2, y, z, 1 - core)
    up = device(x + 1, y, z, core)
    down = device(x - 1, y, z, core)
    nxt = device(x, y, z + 1, core)
    prv = device(x, y, z - 1, core)
    row_far = lax.rem(row + 2, 4)
    row_mate = row_of(x, 1 - core)
    row_mate_far = lax.rem(row_mate + 2, 4)
    row_up = row_of(x + 1, core)
    row_down = row_of(x - 1, core)
    row_up_mate = row_of(x + 1, 1 - core)
    row_down_mate = row_of(x - 1, 1 - core)

    load = pltpu.make_async_copy(front_hbm, slab, load_sem)
    load.start()

    barrier = pltpu.get_barrier_semaphore()
    for target in (mate, far, far_mate, up, down, nxt, prv):
        pl.semaphore_signal(barrier, 1, device_id=target)
    pl.semaphore_wait(barrier, 7)

    def rows(j):
        return pl.ds(2 * STARTS[j], 2 * CHUNKS[j])

    def eight(base):
        return pl.ds(base, 8)

    def remote(src, dst, s, r, dev):
        return pltpu.make_async_remote_copy(src, dst, s, r, device_id=dev)

    def send_x(j):
        pool = pools[j]
        keep = keep_hbm.at[:, rows(j)]
        give = give_hbm.at[:, rows(j)]
        mine = pool.at[eight(8 * row)]
        given = pool.at[eight(32 + 8 * row)]
        return (
            remote(keep, mine, xs.at[0, j], xr.at[0, j], far),
            remote(give, given, xs.at[1, j], xr.at[1, j], up),
            remote(give, given, xs.at[2, j], xr.at[2, j], down),
        )

    def recv_x(j):
        pool = pools[j]
        give = give_hbm.at[:, rows(j)]
        return (
            remote(give, pool.at[eight(8 * row_far)], xs.at[0, j], xr.at[0, j], far),
            remote(give, pool.at[eight(32 + 8 * row_down)], xs.at[1, j], xr.at[1, j], down),
            remote(give, pool.at[eight(32 + 8 * row_up)], xs.at[2, j], xr.at[2, j], up),
        )

    def own_copy(j):
        return pltpu.make_async_copy(
            keep_hbm.at[:, rows(j)], pools[j].at[eight(8 * row)], own_sem.at[j]
        )

    def own_relay(j):
        mine = pools[j].at[eight(8 * row)]
        return remote(keep_hbm.at[:, rows(j)], mine, ms.at[0, j], mr.at[0, j], mate)

    def relays(j):
        out = []
        for p, base in ((1, 8 * row_far), (2, 32 + 8 * row_down), (3, 32 + 8 * row_up)):
            part = pools[j].at[eight(base)]
            out.append(remote(part, part, ms.at[p, j], mr.at[p, j], mate))
        return out

    def relayed(j):
        out = []
        for p, base in (
            (0, 8 * row_mate),
            (1, 8 * row_mate_far),
            (2, 32 + 8 * row_down_mate),
            (3, 32 + 8 * row_up_mate),
        ):
            part = pools[j].at[eight(base)]
            out.append(remote(part, part, ms.at[p, j], mr.at[p, j], mate))
        return out

    def begin_x(j):
        for c in send_x(j):
            c.start()
        own_copy(j).start()
        own_relay(j).start()

    def arrive_x(j):
        for c in recv_x(j):
            c.wait_recv()
        for c in relays(j):
            c.start()

    def assemble(j):
        own_copy(j).wait()
        for c in relayed(j):
            c.wait_recv()
        pool = pools[j]

        def one(b, carry):
            kept = pool[inv[b]]
            moved = pool[inv[32 + b]]
            slab[b, rows(j), :] = slab[b, rows(j), :] + kept + moved
            return carry

        lax.fori_loop(0, 32, one, 0, unroll=4)

    def part(ref, way, t):
        span = 16 // GROUPS
        base = 16 * way + span * (t % GROUPS)
        return ref.at[pl.ds(base, span), pl.ds(pl.multiple_of(16 * (t // GROUPS), 16), 16)]

    def hop(ref, way, t):
        return remote(
            part(ref, way, t),
            part(panel, way, t),
            zs.at[way, t],
            zr.at[way, t],
            prv if way else nxt,
        )

    def early_copy(i):
        return pltpu.make_async_copy((keep_hbm, give_hbm)[i], early.at[i, pl.ds(0, 8)], es.at[i])

    def swap(i):
        return remote(mix.at[2 * i + 1 - core], mix.at[4 + i], bs.at[i], br.at[i], mate)

    lend_keep = remote(mix.at[6], mix.at[0], bs.at[2], br.at[0], nxt)
    lend_give = remote(mix.at[7], mix.at[0], bs.at[3], br.at[0], prv)
    keep_far = remote(mix.at[0], mix.at[1], bs.at[0], br.at[1], far)
    keep_back = remote(mix.at[1], mix.at[8], bs.at[1], br.at[2], prv)
    give_up = remote(mix.at[0], mix.at[1], bs.at[0], br.at[1], up)
    give_down = remote(mix.at[0], mix.at[2], bs.at[1], br.at[2], down)
    give_back = remote(mix.at[3], mix.at[9], bs.at[2], br.at[3], nxt)

    def lend_across():
        @pl.when(z == 1)
        def _():
            lend_keep.wait_recv()
            keep_far.start()

        @pl.when(z == 7)
        def _():
            lend_give.wait_recv()
            give_up.start()
            give_down.start()

    def lend_back():
        @pl.when(z == 1)
        def _():
            keep_far.wait_recv()
            keep_back.start()

        @pl.when(z == 7)
        def _():
            give_up.wait_recv()
            give_down.wait_recv()
            mix[3] = mix[1] + mix[2]
            give_back.start()

    def trade():
        return remote(halves.at[core], halves.at[core], bs.at[5], br.at[5], mate)

    def trade_in():
        return remote(halves.at[1 - core], halves.at[1 - core], bs.at[5], br.at[5], mate)

    def lead_begin():
        for i in (0, 1):
            early_copy(i).wait()
        for i in (0, 1):
            for p in (0, 1):
                mix[2 * i + p] = early[i, inv[64 + 2 * i + p]]
        for i in (0, 1):
            swap(i).start()
        for i in (0, 1):
            swap(i).wait_recv()
        mine = mix[core] + mix[4]
        mix[6] = jnp.where(row < 2, mine + slab[0], mine)
        mix[7] = mix[2 + core] + mix[5]
        lend_keep.start()
        lend_give.start()

    def lead_end():
        keep_back.wait_recv()
        give_back.wait_recv()
        halves[core] = mix[6] + mix[8] + mix[9]
        trade().start()
        trade_in().wait_recv()
        lead = square(halves, 0, 1)
        work[...] = 0.5 * (lead + lead.T)

    def quarter(c, q):
        return inverse.at[pl.ds(pl.multiple_of(128 * c + 64 * q, 64), 64)]

    def extra(way, q):
        ref = quarter(core, q)
        return remote(ref, ref, us.at[way, q], ur.at[q], prv if way else nxt)

    def extra_mate(q):
        ref = quarter(core, q)
        return remote(ref, ref, vs.at[q], vr.at[q], mate)

    def extra_from_mate(q):
        ref = quarter(1 - core, q)
        return remote(ref, ref, vs.at[q], vr.at[q], mate)

    def both_part(ref, d):
        span = 16 // GROUPS
        row8 = ROUND // GROUPS + d // (2 * GROUPS)
        return ref.at[
            pl.ds(span * (d % (2 * GROUPS)), span), pl.ds(pl.multiple_of(16 * row8, 16), 16)
        ]

    def both(ref, way, d):
        return remote(
            both_part(ref, d), both_part(panel, d), ds.at[way, d], dr.at[d], prv if way else nxt
        )

    def row_copy(j, dst):
        return pltpu.make_async_copy(slab.at[:, rows(j)], dst.at[:, rows(j)], row_sem.at[j])

    for j in range(NCH):
        pools[j][64] = jnp.zeros(pools[j].shape[1:], F32)
    lend_across()
    for j in range(WINDOW):
        begin_x(j)
    load.wait()

    @pl.when(z == 0)
    def _():
        for i in (0, 1):
            early_copy(i).start()
            early[i, 8] = jnp.zeros((256, 128), F32)
        lead_begin()
        for j in range(NCH):
            arrive_x(j)
            if j + WINDOW < NCH:
                begin_x(j + WINDOW)
            assemble(j)
            row_copy(j, panel_out).start()

            def launch(t, carry):
                for way in (0, 1):
                    hop(slab, way, t).start()
                return carry

            def launch_both(d, carry):
                for way in (0, 1):
                    both(slab, way, d).start()
                return carry

            first = STARTS[j] // 8 * GROUPS
            end = first + CHUNKS[j] // 8 * GROUPS
            if end <= ROUND:
                lax.fori_loop(first, end, launch, 0)
            else:
                lax.fori_loop(2 * (first - ROUND), 2 * (end - ROUND), launch_both, 0)
            if end == ROUND:
                levels(inverse, upper, *LEVELS[j])
                for way in (0, 1):
                    for q in (0, 1):
                        extra(way, q).start()
                continue
            if j == LEAD_AT:
                lead_end()
            if j in PANELS:
                for p in range(*PANELS[j]):
                    factor_panel(work, upper, 16 * p)
            if j in LEVELS:
                levels(inverse, upper, *LEVELS[j])

    half = z // 2
    owner = 2 * lax.rem(z, 2)

    def cut(k):
        return pl.ds(0, 2 * CUT) if k == 0 else pl.ds(2 * CUT, 256 - 2 * CUT)

    def spread(h, k):
        src = panel.at[half, cut(k)]
        dst = win.at[h, cut(k)]
        return [
            remote(src, dst, ws.at[k, i], wr.at[h, k], dev)
            for i, dev in enumerate((mate, far, far_mate))
        ]

    def panel_copy(k):
        return pltpu.make_async_copy(
            panel.at[:, cut(k)], panel_out.at[:, cut(k)], out_sem.at[k]
        )

    def share(k):
        for h in (0, 1):

            @pl.when(row == owner + h)
            def _():
                for c in spread(h, k):
                    c.start()
                win[h, cut(k), :] = panel[half, cut(k), :]

        panel_copy(k).start()

    @pl.when(z != 0)
    def _():
        total = max(SLOTS + SKEW * 3, ROUND + SKEW * 6)

        def step(s, carry):
            for way in (0, 1):
                lag = (7 - z) if way else (z - 1)
                near = (z > 4) if way else (z <= 4)
                end = 5 if way else 4
                t = s - SKEW * lag

                @pl.when((t >= 0) & (t < ROUND))
                def _():
                    copy = hop(panel, way, t)
                    copy.wait_recv()

                    @pl.when(lag < 6)
                    def _():
                        copy.start()

                @pl.when(near & (t >= ROUND) & (t < SLOTS))
                def _():
                    for q in (0, 1):

                        @pl.when(t == ROUND + q)
                        def _():
                            copy = extra(way, q)
                            copy.wait_recv()

                            @pl.when(z != end)
                            def _():
                                copy.start()

                            extra_mate(q).start()

                    @pl.when(t >= ROUND + 2)
                    def _():
                        copy = both(panel, way, t - ROUND - 2)
                        copy.wait_recv()

                        @pl.when(z != end)
                        def _():
                            copy.start()

            return carry

        lax.fori_loop(0, LEAD_STEP, step, 0)
        lend_back()
        done = LEAD_STEP
        shared = False
        for j in range(NCH):
            until = (STARTS[j] + CHUNKS[j]) // 8 * GROUPS + LATE
            if until >= CUT_AT and not shared:
                lax.fori_loop(done, CUT_AT, step, 0)
                done = CUT_AT
                share(0)
                shared = True
            if until > done:
                lax.fori_loop(done, until, step, 0)
                done = until
            arrive_x(j)
            if j + WINDOW < NCH:
                begin_x(j + WINDOW)
            if j >= BEHIND:
                assemble(j - BEHIND)
                row_copy(j - BEHIND, slab_out).start()
        if not shared:
            lax.fori_loop(done, CUT_AT, step, 0)
            done = CUT_AT
            share(0)
        lax.fori_loop(done, total, step, 0)
        share(1)
        for j in range(max(0, NCH - BEHIND), NCH):
            assemble(j)
            row_copy(j, slab_out).start()

    @pl.when(z == 0)
    def _():
        copy = pltpu.make_async_copy(upper, upper_out, out_sem.at[4])
        copy.start()
        win[...] = jnp.zeros_like(win)
        copy.wait()

    @pl.when(z != 0)
    def _():
        for q in (0, 1):
            extra_from_mate(q).wait_recv()
        for h in (0, 1):

            @pl.when(row != owner + h)
            def _():
                for k in (0, 1):
                    ref = win.at[h, cut(k)]
                    remote(ref, ref, ws.at[k, 0], wr.at[h, k], mate).wait_recv()

    pltpu.make_async_copy(win, window_out, out_sem.at[2]).start()
    pltpu.make_async_copy(inverse, inverse_out, out_sem.at[3]).start()

    @pl.when(z == 0)
    def _():
        for i in (0, 1):
            swap(i).wait_send()
        lend_keep.wait_send()
        lend_give.wait_send()
        trade().wait_send()

    @pl.when(z == 1)
    def _():
        keep_far.wait_send()
        keep_back.wait_send()

    @pl.when(z == 7)
    def _():
        give_up.wait_send()
        give_down.wait_send()
        give_back.wait_send()

    @pl.when(z != 0)
    def _():
        for q in (0, 1):
            extra_mate(q).wait_send()
        for k in (0, 1):
            panel_copy(k).wait()
        for h in (0, 1):

            @pl.when(row == owner + h)
            def _():
                for k in (0, 1):
                    for c in spread(h, k):
                        c.wait_send()

    for way in (0, 1):

        @pl.when(((z == 0) | (z > 5)) if way else (z < 4))
        def _():
            for q in (0, 1):
                extra(way, q).wait_send()

            def drain_both(d, carry):
                both(panel, way, d).wait_send()
                return carry

            lax.fori_loop(0, BOTH, drain_both, 0)

    for j in range(NCH):
        for c in send_x(j):
            c.wait_send()
        own_relay(j).wait_send()
        for c in relays(j):
            c.wait_send()

    def drain(t, carry):
        for way in (0, 1):
            last = 1 if way else 7

            @pl.when(z != last)
            def _():
                hop(panel, way, t).wait_send()

        return carry

    lax.fori_loop(0, ROUND, drain, 0)
    for j in range(NCH):
        row_copy(j, slab_out).wait()
    pltpu.make_async_copy(win, window_out, out_sem.at[2]).wait()
    pltpu.make_async_copy(inverse, inverse_out, out_sem.at[3]).wait()


def exchange(inv, front, keep, give):
    big = jax.ShapeDtypeStruct(front.shape, F32)
    square_shape = jax.ShapeDtypeStruct((256, 256), F32)
    anywhere = pl.BlockSpec(memory_space=pl.ANY)
    dma = pltpu.SemaphoreType.DMA
    return pl.pallas_call(
        exchange_kernel,
        out_shape=[big, big, jax.ShapeDtypeStruct((2, 256, 128), F32), square_shape, square_shape],
        in_specs=[pl.BlockSpec(memory_space=pltpu.SMEM)] + [pl.BlockSpec(memory_space=pltpu.HBM)] * 3,
        out_specs=[anywhere] * 5,
        scratch_shapes=[
            pltpu.VMEM(front.shape, F32),
            pltpu.VMEM(front.shape, F32),
            pltpu.VMEM((2, 256, 128), F32),
            pltpu.VMEM((2, 9, 256, 128), F32),
            pltpu.VMEM((10, 256, 128), F32),
            pltpu.VMEM((2, 256, 128), F32),
            pltpu.VMEM((256, 256), F32),
            pltpu.VMEM((256, 256), F32),
            pltpu.VMEM((256, 256), F32),
            dma,
            dma((NCH,)),
            dma((3, NCH)),
            dma((3, NCH)),
            dma((4, NCH)),
            dma((4, NCH)),
            dma((2, ROUND)),
            dma((2, ROUND)),
            dma((2, 3)),
            dma((2, 2)),
            dma((2,)),
            dma((6,)),
            dma((6,)),
            dma((2, 2)),
            dma((2,)),
            dma((2,)),
            dma((2,)),
            dma((2, BOTH)),
            dma((BOTH,)),
            dma((5,)),
            dma((NCH,)),
        ]
        + [pltpu.VMEM((65, 2 * n, 128), F32) for n in CHUNKS],
        compiler_params=pltpu.CompilerParams(
            collective_id=0, has_side_effects=True, vmem_limit_bytes=40 << 20
        ),
        name="exchange",
    )(inv, front, keep, give)


def three(a):
    hi = a.astype(BF16)
    rest = a - hi.astype(F32)
    mid = rest.astype(BF16)
    low = (rest - mid.astype(F32)).astype(BF16)
    return hi, mid, low


def factor_panel(work, upper, j0, n=16):
    r = work[j0 : j0 + n, :]
    sub = lax.broadcasted_iota(jnp.int32, (n, 128), 0)
    sub2 = lax.broadcasted_iota(jnp.int32, (n, 256), 0)
    lane2 = lax.broadcasted_iota(jnp.int32, (n, 256), 1)
    g = [jnp.broadcast_to(r[:, j0 + i : j0 + i + 1], (n, 128)) for i in range(n)]
    for i in range(n):
        inv = lax.rsqrt(g[i][i : i + 1, :])
        l = g[i] * inv
        below = jnp.where(sub > i, l, 0.0)
        for m in range(i + 1, n):
            g[m] = g[m] - below * l[m : m + 1, :]
        line = r[i : i + 1, :] * jnp.concatenate([inv, inv], axis=1)
        r = jnp.where(sub2 == i, line, r - jnp.concatenate([below, below], axis=1) * line)
    r = jnp.where(lane2 >= sub2 + j0, r, 0.0)
    upper[j0 : j0 + n, :] = r
    if j0 + n < 256:
        h, m, l = three(r)
        a = jnp.concatenate([h, h, m, h, l, m], axis=0)
        b = jnp.concatenate([h, m, h, l, h, m], axis=0)
        t = lax.dot_general(a, b, (((0,), (0,)), ((), ())), preferred_element_type=F32)
        work[j0 + n :, :] = work[j0 + n :, :] - t[j0 + n :, :]


def levels(inverse, upper, first, end):
    i = lax.broadcasted_iota(jnp.int32, (256, 256), 0)
    j = lax.broadcasted_iota(jnp.int32, (256, 256), 1)
    u = upper[...]
    if first == 0:
        inv = jnp.where(i == j, 1.0 / jnp.where(i == j, u, 1.0), 0.0)
    else:
        inv = inverse[...]
    for level in range(first, end):
        s = 1 << level
        off = jnp.where((i // (2 * s) == j // (2 * s)) & (i // s < j // s), u, 0.0)
        step = jnp.dot(inv, off, precision=precise, preferred_element_type=F32)
        inv = inv - jnp.dot(step, inv, precision=precise, preferred_element_type=F32)
    inverse[...] = inv


def square(ref, a, b):
    even, odd = pl.ds(0, 128, 2), pl.ds(1, 128, 2)
    top = jnp.concatenate([ref[a, even, :], ref[a, odd, :]], axis=1)
    low = jnp.concatenate([ref[b, even, :], ref[b, odd, :]], axis=1)
    return jnp.concatenate([top, low], axis=0)


def update_kernel(ids, panel, slab, win, inverse, upper, out, weight, top):
    even, odd = pl.ds(0, TILE, 2), pl.ds(1, TILE, 2)

    @pl.when(pl.program_id(0) == 0)
    def _():
        inv = inverse[...]

        @pl.when(ids[0] == 0)
        def _():
            weight[...] = -inv
            low = upper[...].T
            top[...] = jnp.where(ids[1] == 0, low[:128], low[128:])

        @pl.when(ids[0] != 0)
        def _():
            y = lax.dot_general(
                inv,
                square(win, 0, 1),
                (((0,), (1,)), ((), ())),
                precision=precise,
                preferred_element_type=F32,
            )
            weight[...] = jnp.dot(inv, y, precision=precise, preferred_element_type=F32)
            top[...] = jnp.zeros_like(top)

    a = jnp.concatenate([panel[even, :], panel[odd, :]], axis=1)
    d = jnp.dot(a, weight[...], precision=precise, preferred_element_type=F32)
    out[even, :] = jnp.where(ids[0] != 0, slab[even, :], 0.0) - d[:, :128]
    out[odd, :] = jnp.where(ids[0] != 0, slab[odd, :], 0.0) - d[:, 128:]

    @pl.when((pl.program_id(0) == 0) & (ids[1] < 2))
    def _():
        out[pl.ds(0, 128, 2), :] = top[:, :128]
        out[pl.ds(1, 128, 2), :] = top[:, 128:]


def update(ids, panel, slab, win, inverse, upper):
    tile = pl.BlockSpec((2 * TILE, 128), lambda i: (i, 0))
    whole = pl.BlockSpec((256, 256), lambda i: (0, 0))
    return pl.pallas_call(
        update_kernel,
        grid=(4096 // TILE,),
        out_shape=jax.ShapeDtypeStruct((8192, 128), F32),
        in_specs=[
            pl.BlockSpec(memory_space=pltpu.SMEM),
            tile,
            tile,
            pl.BlockSpec((2, 256, 128), lambda i: (0, 0, 0)),
            whole,
            whole,
        ],
        out_specs=tile,
        scratch_shapes=[pltpu.VMEM((256, 256), F32), pltpu.VMEM((128, 256), F32)],
        compiler_params=pltpu.CompilerParams(vmem_limit_bytes=40 << 20),
        name="update",
    )(ids, panel, slab, win, inverse, upper)


def local(front_slab, child_keep, child_give, map_keep, map_give):
    front_id = lax.axis_index("front")
    row_id = lax.axis_index("row")
    col_id = lax.axis_index("col")
    front, keep, give = (
        pltpu.with_memory_space_constraint(a.reshape(n, 256, 128), pltpu.HBM)
        for a, n in ((front_slab, 32), (child_keep, 8), (child_give, 8))
    )
    kept = lax.dynamic_index_in_dim(map_keep, front_id, 0, keepdims=False)
    moved = lax.dynamic_index_in_dim(map_give, front_id ^ 1, 0, keepdims=False)
    tables = jnp.stack([kept.T.reshape(32), moved.T.reshape(32)])
    parent = jnp.arange(32, dtype=jnp.int32) * 4 + row_id
    slot = jnp.arange(64, dtype=jnp.int32).reshape(2, 1, 32)
    hit = tables[:, None, :] == parent[None, :, None]
    inv = (64 + jnp.sum(jnp.where(hit, slot - 64, 0), axis=2)).reshape(64).astype(jnp.int32)
    ids = jnp.stack([col_id, row_id]).astype(jnp.int32)
    given = lax.dynamic_index_in_dim(map_give, front_id, 0, keepdims=False)
    mine = lax.dynamic_index_in_dim(jnp.stack([kept, given]), row_id, 2, keepdims=False)
    own = jnp.arange(8, dtype=jnp.int32)
    lead = mine[:, None, :] == jnp.arange(2, dtype=jnp.int32)[None, :, None]
    lead = (8 + jnp.sum(jnp.where(lead, own - 8, 0), axis=2)).reshape(4).astype(jnp.int32)
    inv = jnp.concatenate([inv, lead])
    panel, slab, win, inverse, upper = exchange(inv, front, keep, give)
    out = update(ids, panel.reshape(8192, 128), slab.reshape(8192, 128), win, inverse, upper)
    return out.reshape(front_slab.shape)


def solution(mesh):
    spec = P("front", None, "row", None, None, "col", None)
    return jax.shard_map(
        local,
        mesh=mesh,
        in_specs=(spec, spec, spec, P(), P()),
        out_specs=spec,
        check_vma=False,
    )
```

```python
import functools

import jax
import jax.numpy as jnp
from jax import lax
from jax.experimental import pallas as pl
from jax.experimental.pallas import tpu as pltpu
from jax.sharding import PartitionSpec as P

F32 = jnp.float32
BF16 = jnp.bfloat16
precise = lax.Precision.HIGHEST

CHUNKS = (8, 8, 16, 16, 16, 16, 16, 16, 8, 8)
STARTS = tuple(sum(CHUNKS[:i]) for i in range(len(CHUNKS)))
NCH = len(CHUNKS)
WINDOW = 3
TILE = 1024
GROUPS = 4
PARTS = 16 * GROUPS
SKEW = 5
ROUND = 14 * GROUPS
BOTH = 2 * (PARTS - ROUND)
SLOTS = ROUND + 2 + BOTH
CUT = 96
CUT_AT = CUT // 8 * GROUPS + 6 * SKEW
LEAD_AT = 4
LEAD_STEP = 12
PANELS = {4: (0, 5), 5: (5, 10), 6: (10, 16)}
LEVELS = {7: (0, 8)}
LATE = 2 * GROUPS
BEHIND = 1


def place():
    front = lax.axis_index("front")
    row = lax.axis_index("row")
    col = lax.axis_index("col")
    x = (row // 2) * 2 + front % 2
    return x, front // 2, col, row % 2


def device(x, y, z, core):
    x = lax.rem(x + 4, 4)
    z = lax.rem(z + 8, 8)
    return {"front": y * 2 + x % 2, "row": (x // 2) * 2 + core, "col": z}


def row_of(x, core):
    return (lax.rem(x + 4, 4) // 2) * 2 + core


def exchange_kernel(
    inv,
    front_hbm,
    keep_hbm,
    give_hbm,
    panel_out,
    slab_out,
    window_out,
    inverse_out,
    upper_out,
    slab,
    panel,
    win,
    early,
    mix,
    halves,
    work,
    upper,
    inverse,
    load_sem,
    own_sem,
    xs,
    xr,
    ms,
    mr,
    zs,
    zr,
    ws,
    wr,
    es,
    bs,
    br,
    us,
    ur,
    vs,
    vr,
    ds,
    dr,
    out_sem,
    row_sem,
    *pools,
):
    x, y, z, core = place()
    row = row_of(x, core)
    mate = device(x, y, z, 1 - core)
    far = device(x + 2, y, z, core)
    far_mate = device(x + 2, y, z, 1 - core)
    up = device(x + 1, y, z, core)
    down = device(x - 1, y, z, core)
    nxt = device(x, y, z + 1, core)
    prv = device(x, y, z - 1, core)
    row_far = lax.rem(row + 2, 4)
    row_mate = row_of(x, 1 - core)
    row_mate_far = lax.rem(row_mate + 2, 4)
    row_up = row_of(x + 1, core)
    row_down = row_of(x - 1, core)
    row_up_mate = row_of(x + 1, 1 - core)
    row_down_mate = row_of(x - 1, 1 - core)

    load = pltpu.make_async_copy(front_hbm, slab, load_sem)
    load.start()

    barrier = pltpu.get_barrier_semaphore()
    for target in (mate, far, far_mate, up, down, nxt, prv):
        pl.semaphore_signal(barrier, 1, device_id=target)
    pl.semaphore_wait(barrier, 7)

    def rows(j):
        return pl.ds(2 * STARTS[j], 2 * CHUNKS[j])

    def eight(base):
        return pl.ds(base, 8)

    def remote(src, dst, s, r, dev):
        return pltpu.make_async_remote_copy(src, dst, s, r, device_id=dev)

    def send_x(j):
        pool = pools[j]
        keep = keep_hbm.at[:, rows(j)]
        give = give_hbm.at[:, rows(j)]
        mine = pool.at[eight(8 * row)]
        given = pool.at[eight(32 + 8 * row)]
        return (
            remote(keep, mine, xs.at[0, j], xr.at[0, j], far),
            remote(give, given, xs.at[1, j], xr.at[1, j], up),
            remote(give, given, xs.at[2, j], xr.at[2, j], down),
        )

    def recv_x(j):
        pool = pools[j]
        give = give_hbm.at[:, rows(j)]
        return (
            remote(give, pool.at[eight(8 * row_far)], xs.at[0, j], xr.at[0, j], far),
            remote(give, pool.at[eight(32 + 8 * row_down)], xs.at[1, j], xr.at[1, j], down),
            remote(give, pool.at[eight(32 + 8 * row_up)], xs.at[2, j], xr.at[2, j], up),
        )

    def own_copy(j):
        return pltpu.make_async_copy(
            keep_hbm.at[:, rows(j)], pools[j].at[eight(8 * row)], own_sem.at[j]
        )

    def own_relay(j):
        mine = pools[j].at[eight(8 * row)]
        return remote(keep_hbm.at[:, rows(j)], mine, ms.at[0, j], mr.at[0, j], mate)

    def relays(j):
        out = []
        for p, base in ((1, 8 * row_far), (2, 32 + 8 * row_down), (3, 32 + 8 * row_up)):
            part = pools[j].at[eight(base)]
            out.append(remote(part, part, ms.at[p, j], mr.at[p, j], mate))
        return out

    def relayed(j):
        out = []
        for p, base in (
            (0, 8 * row_mate),
            (1, 8 * row_mate_far),
            (2, 32 + 8 * row_down_mate),
            (3, 32 + 8 * row_up_mate),
        ):
            part = pools[j].at[eight(base)]
            out.append(remote(part, part, ms.at[p, j], mr.at[p, j], mate))
        return out

    def begin_x(j):
        for c in send_x(j):
            c.start()
        own_copy(j).start()
        own_relay(j).start()

    def arrive_x(j):
        for c in recv_x(j):
            c.wait_recv()
        for c in relays(j):
            c.start()

    def assemble(j):
        own_copy(j).wait()
        for c in relayed(j):
            c.wait_recv()
        pool = pools[j]

        def one(b, carry):
            kept = pool[inv[b]]
            moved = pool[inv[32 + b]]
            slab[b, rows(j), :] = slab[b, rows(j), :] + kept + moved
            return carry

        lax.fori_loop(0, 32, one, 0, unroll=4)

    def part(ref, way, t):
        span = 16 // GROUPS
        base = 16 * way + span * (t % GROUPS)
        return ref.at[pl.ds(base, span), pl.ds(pl.multiple_of(16 * (t // GROUPS), 16), 16)]

    def hop(ref, way, t):
        return remote(
            part(ref, way, t),
            part(panel, way, t),
            zs.at[way, t],
            zr.at[way, t],
            prv if way else nxt,
        )

    def early_copy(i):
        return pltpu.make_async_copy((keep_hbm, give_hbm)[i], early.at[i, pl.ds(0, 8)], es.at[i])

    def swap(i):
        return remote(mix.at[2 * i + 1 - core], mix.at[4 + i], bs.at[i], br.at[i], mate)

    lend_keep = remote(mix.at[6], mix.at[0], bs.at[2], br.at[0], nxt)
    lend_give = remote(mix.at[7], mix.at[0], bs.at[3], br.at[0], prv)
    keep_far = remote(mix.at[0], mix.at[1], bs.at[0], br.at[1], far)
    keep_back = remote(mix.at[1], mix.at[8], bs.at[1], br.at[2], prv)
    give_up = remote(mix.at[0], mix.at[1], bs.at[0], br.at[1], up)
    give_down = remote(mix.at[0], mix.at[2], bs.at[1], br.at[2], down)
    give_back = remote(mix.at[3], mix.at[9], bs.at[2], br.at[3], nxt)

    def lend_across():
        @pl.when(z == 1)
        def _():
            lend_keep.wait_recv()
            keep_far.start()

        @pl.when(z == 7)
        def _():
            lend_give.wait_recv()
            give_up.start()
            give_down.start()

    def lend_back():
        @pl.when(z == 1)
        def _():
            keep_far.wait_recv()
            keep_back.start()

        @pl.when(z == 7)
        def _():
            give_up.wait_recv()
            give_down.wait_recv()
            mix[3] = mix[1] + mix[2]
            give_back.start()

    def trade():
        return remote(halves.at[core], halves.at[core], bs.at[5], br.at[5], mate)

    def trade_in():
        return remote(halves.at[1 - core], halves.at[1 - core], bs.at[5], br.at[5], mate)

    def lead_begin():
        for i in (0, 1):
            early_copy(i).wait()
        for i in (0, 1):
            for p in (0, 1):
                mix[2 * i + p] = early[i, inv[64 + 2 * i + p]]
        for i in (0, 1):
            swap(i).start()
        for i in (0, 1):
            swap(i).wait_recv()
        mine = mix[core] + mix[4]
        mix[6] = jnp.where(row < 2, mine + slab[0], mine)
        mix[7] = mix[2 + core] + mix[5]
        lend_keep.start()
        lend_give.start()

    def lead_end():
        keep_back.wait_recv()
        give_back.wait_recv()
        halves[core] = mix[6] + mix[8] + mix[9]
        trade().start()
        trade_in().wait_recv()
        lead = square(halves, 0, 1)
        work[...] = 0.5 * (lead + lead.T)

    def quarter(c, q):
        return inverse.at[pl.ds(pl.multiple_of(128 * c + 64 * q, 64), 64)]

    def extra(way, q):
        ref = quarter(core, q)
        return remote(ref, ref, us.at[way, q], ur.at[q], prv if way else nxt)

    def extra_mate(q):
        ref = quarter(core, q)
        return remote(ref, ref, vs.at[q], vr.at[q], mate)

    def extra_from_mate(q):
        ref = quarter(1 - core, q)
        return remote(ref, ref, vs.at[q], vr.at[q], mate)

    def both_part(ref, d):
        span = 16 // GROUPS
        row8 = ROUND // GROUPS + d // (2 * GROUPS)
        return ref.at[
            pl.ds(span * (d % (2 * GROUPS)), span), pl.ds(pl.multiple_of(16 * row8, 16), 16)
        ]

    def both(ref, way, d):
        return remote(
            both_part(ref, d), both_part(panel, d), ds.at[way, d], dr.at[d], prv if way else nxt
        )

    def row_copy(j, dst):
        return pltpu.make_async_copy(slab.at[:, rows(j)], dst.at[:, rows(j)], row_sem.at[j])

    for j in range(NCH):
        pools[j][64] = jnp.zeros(pools[j].shape[1:], F32)
    lend_across()
    for j in range(WINDOW):
        begin_x(j)
    load.wait()

    @pl.when(z == 0)
    def _():
        for i in (0, 1):
            early_copy(i).start()
            early[i, 8] = jnp.zeros((256, 128), F32)
        lead_begin()
        for j in range(NCH):
            arrive_x(j)
            if j + WINDOW < NCH:
                begin_x(j + WINDOW)
            assemble(j)
            row_copy(j, panel_out).start()

            def launch(t, carry):
                for way in (0, 1):
                    hop(slab, way, t).start()
                return carry

            def launch_both(d, carry):
                for way in (0, 1):
                    both(slab, way, d).start()
                return carry

            first = STARTS[j] // 8 * GROUPS
            end = first + CHUNKS[j] // 8 * GROUPS
            if end <= ROUND:
                lax.fori_loop(first, end, launch, 0)
            else:
                lax.fori_loop(2 * (first - ROUND), 2 * (end - ROUND), launch_both, 0)
            if end == ROUND:
                levels(inverse, upper, *LEVELS[j])
                for way in (0, 1):
                    for q in (0, 1):
                        extra(way, q).start()
                continue
            if j == LEAD_AT:
                lead_end()
            if j in PANELS:
                for p in range(*PANELS[j]):
                    factor_panel(work, upper, 16 * p)
            if j in LEVELS:
                levels(inverse, upper, *LEVELS[j])

    half = z // 2
    owner = 2 * lax.rem(z, 2)

    def cut(k):
        return pl.ds(0, 2 * CUT) if k == 0 else pl.ds(2 * CUT, 256 - 2 * CUT)

    def spread(h, k):
        src = panel.at[half, cut(k)]
        dst = win.at[h, cut(k)]
        return [
            remote(src, dst, ws.at[k, i], wr.at[h, k], dev)
            for i, dev in enumerate((mate, far, far_mate))
        ]

    def panel_copy(k):
        return pltpu.make_async_copy(
            panel.at[:, cut(k)], panel_out.at[:, cut(k)], out_sem.at[k]
        )

    def share(k):
        for h in (0, 1):

            @pl.when(row == owner + h)
            def _():
                for c in spread(h, k):
                    c.start()
                win[h, cut(k), :] = panel[half, cut(k), :]

        panel_copy(k).start()

    @pl.when(z != 0)
    def _():
        total = max(SLOTS + SKEW * 3, ROUND + SKEW * 6)

        def step(s, carry):
            for way in (0, 1):
                lag = (7 - z) if way else (z - 1)
                near = (z > 4) if way else (z <= 4)
                end = 5 if way else 4
                t = s - SKEW * lag

                @pl.when((t >= 0) & (t < ROUND))
                def _():
                    copy = hop(panel, way, t)
                    copy.wait_recv()

                    @pl.when(lag < 6)
                    def _():
                        copy.start()

                @pl.when(near & (t >= ROUND) & (t < SLOTS))
                def _():
                    for q in (0, 1):

                        @pl.when(t == ROUND + q)
                        def _():
                            copy = extra(way, q)
                            copy.wait_recv()

                            @pl.when(z != end)
                            def _():
                                copy.start()

                            extra_mate(q).start()

                    @pl.when(t >= ROUND + 2)
                    def _():
                        copy = both(panel, way, t - ROUND - 2)
                        copy.wait_recv()

                        @pl.when(z != end)
                        def _():
                            copy.start()

            return carry

        lax.fori_loop(0, LEAD_STEP, step, 0)
        lend_back()
        done = LEAD_STEP
        shared = False
        for j in range(NCH):
            until = (STARTS[j] + CHUNKS[j]) // 8 * GROUPS + LATE
            if until >= CUT_AT and not shared:
                lax.fori_loop(done, CUT_AT, step, 0)
                done = CUT_AT
                share(0)
                shared = True
            if until > done:
                lax.fori_loop(done, until, step, 0)
                done = until
            arrive_x(j)
            if j + WINDOW < NCH:
                begin_x(j + WINDOW)
            if j >= BEHIND:
                assemble(j - BEHIND)
                row_copy(j - BEHIND, slab_out).start()
        if not shared:
            lax.fori_loop(done, CUT_AT, step, 0)
            done = CUT_AT
            share(0)
        lax.fori_loop(done, total, step, 0)
        share(1)
        for j in range(max(0, NCH - BEHIND), NCH):
            assemble(j)
            row_copy(j, slab_out).start()

    @pl.when(z == 0)
    def _():
        copy = pltpu.make_async_copy(upper, upper_out, out_sem.at[4])
        copy.start()
        win[...] = jnp.zeros_like(win)
        copy.wait()

    @pl.when(z != 0)
    def _():
        for q in (0, 1):
            extra_from_mate(q).wait_recv()
        u = inverse[...]
        work[...] = lax.dot_general(
            u, u, (((1,), (1,)), ((), ())), precision=precise, preferred_element_type=F32
        )
        for h in (0, 1):

            @pl.when(row != owner + h)
            def _():
                for k in (0, 1):
                    ref = win.at[h, cut(k)]
                    remote(ref, ref, ws.at[k, 0], wr.at[h, k], mate).wait_recv()

    pltpu.make_async_copy(win, window_out, out_sem.at[2]).start()

    @pl.when(z == 0)
    def _():
        pltpu.make_async_copy(inverse, inverse_out, out_sem.at[3]).start()

    @pl.when(z != 0)
    def _():
        pltpu.make_async_copy(work, inverse_out, out_sem.at[3]).start()


    @pl.when(z == 0)
    def _():
        for i in (0, 1):
            swap(i).wait_send()
        lend_keep.wait_send()
        lend_give.wait_send()
        trade().wait_send()

    @pl.when(z == 1)
    def _():
        keep_far.wait_send()
        keep_back.wait_send()

    @pl.when(z == 7)
    def _():
        give_up.wait_send()
        give_down.wait_send()
        give_back.wait_send()

    @pl.when(z != 0)
    def _():
        for q in (0, 1):
            extra_mate(q).wait_send()
        for k in (0, 1):
            panel_copy(k).wait()
        for h in (0, 1):

            @pl.when(row == owner + h)
            def _():
                for k in (0, 1):
                    for c in spread(h, k):
                        c.wait_send()

    for way in (0, 1):

        @pl.when(((z == 0) | (z > 5)) if way else (z < 4))
        def _():
            for q in (0, 1):
                extra(way, q).wait_send()

            def drain_both(d, carry):
                both(panel, way, d).wait_send()
                return carry

            lax.fori_loop(0, BOTH, drain_both, 0)

    for j in range(NCH):
        for c in send_x(j):
            c.wait_send()
        own_relay(j).wait_send()
        for c in relays(j):
            c.wait_send()

    def drain(t, carry):
        for way in (0, 1):
            last = 1 if way else 7

            @pl.when(z != last)
            def _():
                hop(panel, way, t).wait_send()

        return carry

    lax.fori_loop(0, ROUND, drain, 0)
    for j in range(NCH):
        row_copy(j, slab_out).wait()
    pltpu.make_async_copy(win, window_out, out_sem.at[2]).wait()
    pltpu.make_async_copy(inverse, inverse_out, out_sem.at[3]).wait()


def exchange(inv, front, keep, give):
    big = jax.ShapeDtypeStruct(front.shape, F32)
    square_shape = jax.ShapeDtypeStruct((256, 256), F32)
    anywhere = pl.BlockSpec(memory_space=pl.ANY)
    dma = pltpu.SemaphoreType.DMA
    return pl.pallas_call(
        exchange_kernel,
        out_shape=[big, big, jax.ShapeDtypeStruct((2, 256, 128), F32), square_shape, square_shape],
        in_specs=[pl.BlockSpec(memory_space=pltpu.SMEM)] + [pl.BlockSpec(memory_space=pltpu.HBM)] * 3,
        out_specs=[anywhere] * 5,
        scratch_shapes=[
            pltpu.VMEM(front.shape, F32),
            pltpu.VMEM(front.shape, F32),
            pltpu.VMEM((2, 256, 128), F32),
            pltpu.VMEM((2, 9, 256, 128), F32),
            pltpu.VMEM((10, 256, 128), F32),
            pltpu.VMEM((2, 256, 128), F32),
            pltpu.VMEM((256, 256), F32),
            pltpu.VMEM((256, 256), F32),
            pltpu.VMEM((256, 256), F32),
            dma,
            dma((NCH,)),
            dma((3, NCH)),
            dma((3, NCH)),
            dma((4, NCH)),
            dma((4, NCH)),
            dma((2, ROUND)),
            dma((2, ROUND)),
            dma((2, 3)),
            dma((2, 2)),
            dma((2,)),
            dma((6,)),
            dma((6,)),
            dma((2, 2)),
            dma((2,)),
            dma((2,)),
            dma((2,)),
            dma((2, BOTH)),
            dma((BOTH,)),
            dma((5,)),
            dma((NCH,)),
        ]
        + [pltpu.VMEM((65, 2 * n, 128), F32) for n in CHUNKS],
        compiler_params=pltpu.CompilerParams(
            collective_id=0, has_side_effects=True, vmem_limit_bytes=40 << 20
        ),
        name="exchange",
    )(inv, front, keep, give)


def three(a):
    hi = a.astype(BF16)
    rest = a - hi.astype(F32)
    mid = rest.astype(BF16)
    low = (rest - mid.astype(F32)).astype(BF16)
    return hi, mid, low


def factor_panel(work, upper, j0, n=16):
    r = work[j0 : j0 + n, :]
    sub = lax.broadcasted_iota(jnp.int32, (n, 128), 0)
    sub2 = lax.broadcasted_iota(jnp.int32, (n, 256), 0)
    lane2 = lax.broadcasted_iota(jnp.int32, (n, 256), 1)
    g = [jnp.broadcast_to(r[:, j0 + i : j0 + i + 1], (n, 128)) for i in range(n)]
    for i in range(n):
        inv = lax.rsqrt(g[i][i : i + 1, :])
        l = g[i] * inv
        below = jnp.where(sub > i, l, 0.0)
        for m in range(i + 1, n):
            g[m] = g[m] - below * l[m : m + 1, :]
        line = r[i : i + 1, :] * jnp.concatenate([inv, inv], axis=1)
        r = jnp.where(sub2 == i, line, r - jnp.concatenate([below, below], axis=1) * line)
    r = jnp.where(lane2 >= sub2 + j0, r, 0.0)
    upper[j0 : j0 + n, :] = r
    if j0 + n < 256:
        h, m, l = three(r)
        a = jnp.concatenate([h, h, m, h, l, m], axis=0)
        b = jnp.concatenate([h, m, h, l, h, m], axis=0)
        t = lax.dot_general(a, b, (((0,), (0,)), ((), ())), preferred_element_type=F32)
        work[j0 + n :, :] = work[j0 + n :, :] - t[j0 + n :, :]


def levels(inverse, upper, first, end):
    i = lax.broadcasted_iota(jnp.int32, (256, 256), 0)
    j = lax.broadcasted_iota(jnp.int32, (256, 256), 1)
    u = upper[...]
    if first == 0:
        inv = jnp.where(i == j, 1.0 / jnp.where(i == j, u, 1.0), 0.0)
    else:
        inv = inverse[...]
    for level in range(first, end):
        s = 1 << level
        off = jnp.where((i // (2 * s) == j // (2 * s)) & (i // s < j // s), u, 0.0)
        step = jnp.dot(inv, off, precision=precise, preferred_element_type=F32)
        inv = inv - jnp.dot(step, inv, precision=precise, preferred_element_type=F32)
    inverse[...] = inv


def square(ref, a, b):
    even, odd = pl.ds(0, 128, 2), pl.ds(1, 128, 2)
    top = jnp.concatenate([ref[a, even, :], ref[a, odd, :]], axis=1)
    low = jnp.concatenate([ref[b, even, :], ref[b, odd, :]], axis=1)
    return jnp.concatenate([top, low], axis=0)


def update_kernel(ids, panel, slab, win, inverse, upper, out, weight, top):
    even, odd = pl.ds(0, TILE, 2), pl.ds(1, TILE, 2)

    @pl.when(pl.program_id(0) == 0)
    def _():
        inv = inverse[...]

        @pl.when(ids[0] == 0)
        def _():
            weight[...] = -inv
            low = upper[...].T
            top[...] = jnp.where(ids[1] == 0, low[:128], low[128:])

        @pl.when(ids[0] != 0)
        def _():
            weight[...] = lax.dot_general(
                inv,
                square(win, 0, 1),
                (((1,), (1,)), ((), ())),
                precision=precise,
                preferred_element_type=F32,
            )
            top[...] = jnp.zeros_like(top)

    a = jnp.concatenate([panel[even, :], panel[odd, :]], axis=1)
    d = jnp.dot(a, weight[...], precision=precise, preferred_element_type=F32)
    out[even, :] = jnp.where(ids[0] != 0, slab[even, :], 0.0) - d[:, :128]
    out[odd, :] = jnp.where(ids[0] != 0, slab[odd, :], 0.0) - d[:, 128:]

    @pl.when((pl.program_id(0) == 0) & (ids[1] < 2))
    def _():
        out[pl.ds(0, 128, 2), :] = top[:, :128]
        out[pl.ds(1, 128, 2), :] = top[:, 128:]


def update(ids, panel, slab, win, inverse, upper):
    tile = pl.BlockSpec((2 * TILE, 128), lambda i: (i, 0))
    whole = pl.BlockSpec((256, 256), lambda i: (0, 0))
    return pl.pallas_call(
        update_kernel,
        grid=(4096 // TILE,),
        out_shape=jax.ShapeDtypeStruct((8192, 128), F32),
        in_specs=[
            pl.BlockSpec(memory_space=pltpu.SMEM),
            tile,
            tile,
            pl.BlockSpec((2, 256, 128), lambda i: (0, 0, 0)),
            whole,
            whole,
        ],
        out_specs=tile,
        scratch_shapes=[pltpu.VMEM((256, 256), F32), pltpu.VMEM((128, 256), F32)],
        compiler_params=pltpu.CompilerParams(vmem_limit_bytes=40 << 20),
        name="update",
    )(ids, panel, slab, win, inverse, upper)


def local(front_slab, child_keep, child_give, map_keep, map_give):
    front_id = lax.axis_index("front")
    row_id = lax.axis_index("row")
    col_id = lax.axis_index("col")
    front, keep, give = (
        pltpu.with_memory_space_constraint(a.reshape(n, 256, 128), pltpu.HBM)
        for a, n in ((front_slab, 32), (child_keep, 8), (child_give, 8))
    )
    kept = lax.dynamic_index_in_dim(map_keep, front_id, 0, keepdims=False)
    moved = lax.dynamic_index_in_dim(map_give, front_id ^ 1, 0, keepdims=False)
    tables = jnp.stack([kept.T.reshape(32), moved.T.reshape(32)])
    parent = jnp.arange(32, dtype=jnp.int32) * 4 + row_id
    slot = jnp.arange(64, dtype=jnp.int32).reshape(2, 1, 32)
    hit = tables[:, None, :] == parent[None, :, None]
    inv = (64 + jnp.sum(jnp.where(hit, slot - 64, 0), axis=2)).reshape(64).astype(jnp.int32)
    ids = jnp.stack([col_id, row_id]).astype(jnp.int32)
    given = lax.dynamic_index_in_dim(map_give, front_id, 0, keepdims=False)
    mine = lax.dynamic_index_in_dim(jnp.stack([kept, given]), row_id, 2, keepdims=False)
    own = jnp.arange(8, dtype=jnp.int32)
    lead = mine[:, None, :] == jnp.arange(2, dtype=jnp.int32)[None, :, None]
    lead = (8 + jnp.sum(jnp.where(lead, own - 8, 0), axis=2)).reshape(4).astype(jnp.int32)
    inv = jnp.concatenate([inv, lead])
    panel, slab, win, inverse, upper = exchange(inv, front, keep, give)
    out = update(ids, panel.reshape(8192, 128), slab.reshape(8192, 128), win, inverse, upper)
    return out.reshape(front_slab.shape)


def solution(mesh):
    spec = P("front", None, "row", None, None, "col", None)
    return jax.shard_map(
        local,
        mesh=mesh,
        in_specs=(spec, spec, spec, P(), P()),
        out_specs=spec,
        check_vma=False,
    )
```
